512 devices in a mesh: leaf: 64 (over x, y, core), grp: 8 (over z).
Axes of the slice: x: 4, y: 8, z: 8, core: 2. Of those that a mesh axis runs over, the one named last changes fastest.
Arguments:
- signal: bfloat16 [64, 2097152], P(None, ('leaf', 'grp')), may hold values from -6 to 6
- points: bfloat16 [3, 2097152], P(None, ('leaf', 'grp')), may hold values from 0 to 1
- basis: bfloat16 [4096, 512, 128], P(('leaf', 'grp')), may hold values from -0.25 to 0.25
- transfer: bfloat16 [4096, 128, 128], P(('leaf', 'grp')), may hold values from -0.5 to 0.5
- leaf_src: int32 [4096, 8], P(('leaf', 'grp')), may hold values from 0 to 63, as said below
- leaf_count: int32 [4096], P(('leaf', 'grp')), may hold values from 1 to 8, as said below
- leaf_blocks: bfloat16 [4096, 8, 128, 128], P(('leaf', 'grp')), may hold values from -0.25 to 0.25
- cluster_src: int32 [64, 16], P('leaf', 'grp'), may hold values from 0 to 63, as said below
- cluster_count: int32 [64], P('leaf'), may hold values from 1 to 16, as said below
- cluster_blocks: bfloat16 [64, 16, 128, 128], P('leaf', 'grp'), may hold values from -0.03125 to 0.03125
Outputs:
- output: bfloat16 [64, 2097152], P(None, ('leaf', 'grp'))
The draws below stay inside these ranges and needn't reach their ends.
Inputs may be any that keep to these rules, and one draw needn't show every extreme that they name: `leaf_src`: each row holds distinct leaves; for leaf number a within its cluster every entry differs from a by 3 to 64 - 3 modulo 64. Slots at or beyond leaf_count hold valid numbers that are not used. `leaf_count`: some leaf uses all 8 slots and some uses one in every draw. `cluster_src`: each row holds distinct clusters, none equal to the row's own cluster. Slots at or beyond cluster_count hold valid numbers that are not used. `cluster_count`: some cluster uses all 16 slots and some uses one in every draw.
All inputs are finite; a program needn't handle non-finite values.
Results may differ from the reference program's by a relative error of at most 0.02.
Values may be sent and summed in bfloat16 or wider, within the bound.
A program may use at most 64 MiB of HBM per device.

```python
import math
import jax
import jax.numpy as jnp
from jax import lax

NB = 512
RK = 128
NV = 64
LD = 8
KL = 8
REACH = 2
LEAVES = 4096
NPTS = 2097152
CLUSTERS = 64
KB = 16
N_LEAF = 64
N_GRP = 8


def draw_leaf_src(key, part):
    key = jax.random.fold_in(key, 11)
    group_size = LD * N_GRP
    choices_n = group_size - 5
    scores = jax.random.randint(key, (LEAVES, choices_n), 0, 1 << 20) * choices_n + jnp.arange(choices_n, dtype=jnp.int32)[None, :]
    ranking = jnp.argsort(scores, axis=1)
    offsets = ranking[:, :KL].astype(jnp.int32) + 3
    position = (jnp.arange(LEAVES, dtype=jnp.int32) % group_size)[:, None]
    return ((position + offsets) % group_size).astype(jnp.int32)


def draw_leaf_count(key, part):
    key = jax.random.fold_in(key, 12)
    first_key, second_key = jax.random.split(key)
    light_count = jax.random.randint(first_key, (LEAVES,), 1, KL // 4 + 1)
    dense_leaf = jax.random.randint(second_key, (LEAVES,), 0, 4) == 0
    counts = jnp.where(dense_leaf, KL, light_count)
    leaf_ids = jnp.arange(LEAVES, dtype=jnp.int32)
    counts = jnp.where(leaf_ids == 0, KL, counts)
    counts = jnp.where(leaf_ids == 1, 1, counts)
    return counts.astype(jnp.int32)


def draw_cluster_src(key, part):
    key = jax.random.fold_in(key, 13)
    choices_n = CLUSTERS - 2
    scores = jax.random.randint(key, (CLUSTERS, choices_n), 0, 1 << 20) * choices_n + jnp.arange(choices_n, dtype=jnp.int32)[None, :]
    ranking = jnp.argsort(scores, axis=1)
    rest = ranking[:, :KB - 1].astype(jnp.int32) + 1
    first = jnp.full((CLUSTERS, 1), CLUSTERS - 1, jnp.int32)
    offsets = jnp.concatenate([first, rest], axis=1)
    position = jnp.arange(CLUSTERS, dtype=jnp.int32)[:, None]
    return ((position + offsets) % CLUSTERS).astype(jnp.int32)


def draw_cluster_count(key, part):
    key = jax.random.fold_in(key, 14)
    counts = jax.random.randint(key, (CLUSTERS,), 1, KB + 1)
    cluster_ids = jnp.arange(CLUSTERS, dtype=jnp.int32)
    counts = jnp.where(cluster_ids == 0, KB, counts)
    counts = jnp.where(cluster_ids == 1, 1, counts)
    return counts.astype(jnp.int32)


def block_levels(rng, shape, cuts, smallest, largest):
    loudness, own = 1.0, jax.random.fold_in(rng, 6)
    for axis_at, blocks in cuts:
        draws = jnp.exp(jax.random.uniform(jax.random.fold_in(own, axis_at), (blocks,), jnp.float32, smallest / len(cuts), largest / len(cuts)))
        loudness = loudness * jnp.repeat(draws, shape[axis_at] // blocks).reshape([-1 if axis == axis_at else 1 for axis in range(len(shape))])
    return loudness


def gaussian(own_key, dims, width, limit, cuts=(), held_as=jnp.bfloat16):
    gain = block_levels(own_key, dims, cuts, -0.22, 0.18) if cuts else 1.0
    drawn = jax.random.normal(own_key, dims, jnp.float32) * width * gain
    return jnp.minimum(jnp.maximum(drawn, -limit), limit).astype(held_as)


def setup_inputs(seed: int = 0) -> dict:
    splits = jax.random.split(jax.random.key(seed), 11)
    signal = gaussian(splits[0], (NV, NPTS), 1.0, 6.0, ((1, 512),))
    points = jnp.clip(1.0 * jax.random.uniform(splits[1], (3, NPTS), jnp.float32) ** block_levels(splits[1], (3, NPTS), ((1, 512),), -0.2, 0.2), 0.0, 1.0).astype(jnp.bfloat16)
    basis = gaussian(splits[2], (LEAVES, NB, RK), NB ** -0.5, 0.25, ((0, 512),))
    transfer = gaussian(splits[3], (LEAVES, RK, RK), RK ** -0.5, 0.5, ((0, 512),))
    leaf_src = draw_leaf_src(jax.random.fold_in(splits[10], 71), 0)
    leaf_count = draw_leaf_count(jax.random.fold_in(splits[10], 71), 0)
    leaf_blocks = gaussian(splits[6], (LEAVES, KL, RK, RK), (4 * RK) ** -0.5, 0.25, ((0, 512),))
    cluster_src = draw_cluster_src(jax.random.fold_in(splits[10], 71), 0)
    cluster_count = draw_cluster_count(jax.random.fold_in(splits[10], 71), 0)
    cluster_blocks = gaussian(splits[9], (CLUSTERS, KB, RK, RK), (4 * RK * LD * N_GRP) ** -0.5, 0.03125, ((0, 64), (1, 8)))
    return dict(signal=signal, points=points, basis=basis, transfer=transfer, leaf_src=leaf_src, leaf_count=leaf_count, leaf_blocks=leaf_blocks, cluster_src=cluster_src, cluster_count=cluster_count, cluster_blocks=cluster_blocks)


softening = 0.0025

def near_block(padded, basis_leaf, field_leaf, first_col):
    extent = (2 * REACH + 1) * NB
    kernel_scale = 0.5 / math.sqrt(extent)
    slice_span = lax.dynamic_slice_in_dim(padded, first_col, extent, 1)
    target = lax.dynamic_slice_in_dim(padded, first_col + REACH * NB, NB, 1)[:3].astype(jnp.float32)
    source = slice_span[:3].astype(jnp.float32)
    distance = jnp.zeros((extent, NB), jnp.float32)
    for axis_id in range(3):
        offset = source[axis_id][:, None] - target[axis_id][None, :]
        distance = distance + offset * offset
    kernel = (kernel_scale * lax.rsqrt(distance + softening)).astype(jnp.bfloat16)
    near_part = jnp.dot(slice_span[3:], kernel, preferred_element_type=jnp.float32)
    far_part = jnp.dot(field_leaf, basis_leaf.T, preferred_element_type=jnp.float32)
    return (near_part + far_part).astype(jnp.bfloat16)

def reference(signal, points, basis, transfer, leaf_src, leaf_count, leaf_blocks, cluster_src, cluster_count, cluster_blocks):
    group_size = LD * N_GRP
    clusters = N_LEAF
    total_leaves = basis.shape[0]
    vector_rows = signal.shape[0]
    by_cluster = signal.reshape(vector_rows, clusters, group_size, NB).transpose(1, 0, 2, 3)
    basis_groups = basis.reshape(clusters, group_size, NB, RK)
    transfer_sets = transfer.reshape(clusters, group_size, RK, RK)

    def upward_one(segment_list):
        signal_block, basis_block, transfer_tile = segment_list
        coefs_block = jnp.einsum('vgn,gnr->gvr', signal_block.astype(jnp.float32), basis_block.astype(jnp.float32)).astype(jnp.bfloat16)
        summed = jnp.einsum('gvr,grs->vs', coefs_block.astype(jnp.float32), transfer_tile.astype(jnp.float32)).astype(jnp.bfloat16)
        return (coefs_block, summed)
    leaf_coefs, cluster_coefs = lax.map(upward_one, (by_cluster, basis_groups, transfer_sets))
    slot_ids = jnp.arange(cluster_src.shape[1], dtype=jnp.int32)
    alive = slot_ids[None, :] < cluster_count[:, None]
    picked = jnp.where(alive[:, :, None, None], cluster_coefs[cluster_src], jnp.zeros((), cluster_coefs.dtype))
    cluster_field = jnp.einsum('ckvr,ckrs->cvs', picked.astype(jnp.float32), cluster_blocks.astype(jnp.float32)).astype(jnp.bfloat16)

    def downward_one(segment_list):
        coefs_block, field_tile, transfer_tile, src_block, count_block, blocks_block = segment_list
        downward_sweep = jnp.einsum('hf,irf->ihr', field_tile.astype(jnp.float32), transfer_tile.astype(jnp.float32))
        slot_live = jnp.arange(src_block.shape[1], dtype=jnp.int32)[None, :] < count_block[:, None]
        sources = jnp.where(slot_live[:, :, None, None], coefs_block[src_block], jnp.zeros((), coefs_block.dtype))
        across = jnp.einsum('gkvr,gkrs->gvs', sources.astype(jnp.float32), blocks_block.astype(jnp.float32))
        return (downward_sweep + across).astype(jnp.bfloat16)
    leaf_field = lax.map(downward_one, (leaf_coefs, cluster_field, transfer_sets, leaf_src.reshape(clusters, group_size, KL), leaf_count.reshape(clusters, group_size), leaf_blocks.reshape(clusters, group_size, KL, RK, RK)))
    leaf_field = leaf_field.reshape(total_leaves, vector_rows, RK)
    stacked = jnp.concatenate([points, signal], axis=0)
    padded = jnp.pad(stacked, ((0, 0), (REACH * NB, REACH * NB)))

    def leaf_out(leaf_index):
        basis_leaf = lax.dynamic_index_in_dim(basis, leaf_index, 0, keepdims=False)
        field_leaf = lax.dynamic_index_in_dim(leaf_field, leaf_index, 0, keepdims=False)
        return near_block(padded, basis_leaf, field_leaf, leaf_index * NB)
    results = lax.map(leaf_out, jnp.arange(total_leaves, dtype=jnp.int32))
    return results.transpose(1, 0, 2).reshape(vector_rows, total_leaves * NB)
```

```python
import functools
import math

import jax
import jax.numpy as jnp
from jax import lax
from jax.experimental import pallas as pl
from jax.experimental.pallas import tpu as pltpu
from jax.sharding import PartitionSpec as P

BF = jnp.bfloat16
F32 = jnp.float32
MESH = pl.DeviceIdType.MESH
SOFTENING = 0.0025
LOW = 16


def split3(value):
    first = value.astype(BF).astype(F32)
    rest = value - first
    second = rest.astype(BF).astype(F32)
    return first, second, rest - second


def dot(a, b, contract=((1,), (0,))):
    return lax.dot_general(a, b, (contract, ((), ())), preferred_element_type=F32)


def kernel(
    n_leaf,
    n_grp,
    low,
    signal,
    points,
    basis,
    transfer,
    leaf_src,
    leaf_count,
    leaf_blocks,
    cluster_src,
    cluster_count,
    cluster_blocks,
    out,
    sig,
    feat,
    feat_t,
    base,
    trans,
    blocks,
    coefs,
    acc,
    result,
    part_t,
    reduce_in,
    up,
    own_blocks,
    send_blocks,
    all_blocks,
    send_src,
    all_src,
    src_smem,
    part,
    field_in,
    field,
    load_sem,
    halo_send,
    halo_recv,
    ring_send,
    ring_recv,
    block_send,
    block_recv,
    src_send,
    src_recv,
    reduce_send,
    reduce_recv,
    low_send,
    low_recv,
    high_send,
    high_recv,
    fred_send,
    fred_recv,
    fgat_send,
    fgat_recv,
    smem_sem,
    store_sem,
):
    leaf = lax.axis_index("leaf")
    grp = lax.axis_index("grp")
    rows, cols = signal.shape
    leaves, width, rank = basis.shape
    slots = leaf_blocks.shape[1]
    mine = cluster_blocks.shape[0]
    rslice = rank // n_grp
    vslice = rows // n_grp
    high = n_leaf // low
    half = n_grp // 2
    edge = 2 * width
    extent = 5 * width
    my_low = lax.rem(leaf, low)
    my_high = leaf // low
    rank_id = leaf * n_grp + grp
    total = n_leaf * n_grp
    right_id = lax.rem(rank_id + 1, total)
    left_id = lax.rem(rank_id + total - 1, total)
    right = (right_id // n_grp, lax.rem(right_id, n_grp))
    left = (left_id // n_grp, lax.rem(left_id, n_grp))

    def grp_peer(i):
        return (leaf, lax.rem(grp + i, n_grp))

    def grp_from(i):
        return lax.rem(grp + n_grp - i, n_grp)

    def low_peer(i):
        return (my_high * low + lax.rem(my_low + i, low), grp)

    def low_from(i):
        return my_high * low + lax.rem(my_low + low - i, low)

    def high_peer(i):
        return (lax.rem(my_high + i, high) * low + my_low, grp)

    def high_from(i):
        return lax.rem(my_high + high - i, high)

    def each(n, fn):
        def body(i, carry):
            fn(i)
            return carry

        lax.fori_loop(1, n, body, 0)

    barrier = pltpu.get_barrier_semaphore()

    def greet(device):
        pl.semaphore_signal(barrier, inc=1, device_id=device, device_id_type=MESH)

    greet(left)
    greet(right)
    each(n_grp, lambda i: greet(grp_peer(i)))
    each(low, lambda i: greet(low_peer(i)))
    each(high, lambda i: greet(high_peer(i)))

    loads = [
        pltpu.make_async_copy(signal, sig.at[:, pl.ds(edge, cols)], load_sem.at[0]),
        pltpu.make_async_copy(basis, base, load_sem.at[1]),
        pltpu.make_async_copy(cluster_blocks, own_blocks, load_sem.at[2]),
        pltpu.make_async_copy(transfer, trans, load_sem.at[3]),
        pltpu.make_async_copy(leaf_blocks, blocks, load_sem.at[4]),
    ]
    for load in loads:
        load.start()

    pts = points[...].astype(F32)
    norm = pts[0:1] * pts[0:1] + pts[1:2] * pts[1:2] + pts[2:3] * pts[2:3]
    pieces = jnp.concatenate(split3(norm), axis=0)
    ones = jnp.ones((3, cols), F32)
    soft = jnp.concatenate(split3(jnp.full((1, cols), SOFTENING, F32)), axis=0)
    fill = jnp.zeros((4, cols), F32)
    feat[:, edge : edge + cols] = jnp.concatenate(
        [-2.0 * pts, ones, pieces, ones, fill], axis=0
    ).astype(BF)
    feat_t[...] = jnp.concatenate([pts, pieces, ones, soft, fill], axis=0).T.astype(BF)
    acc[...] = jnp.zeros_like(acc)
    src_row = lax.broadcasted_iota(jnp.int32, (8, 128), 0)
    packed_src = jnp.zeros((8, 128), jnp.int32)
    for i in range(mine):
        packed_src = jnp.where(src_row == i, cluster_src[0, i], packed_src)
    send_src[...] = packed_src
    all_src[grp] = packed_src
    loads[2].wait()
    for i in range(mine):
        alive = (grp * mine + i) < cluster_count[0]
        keep = jnp.where(alive, 1.0, 0.0)
        send_blocks[i] = (own_blocks[i].astype(F32) * keep).astype(BF)

    pl.semaphore_wait(barrier, n_grp - 1 + low - 1 + high - 1 + 2)

    def halo_copies():
        return [
            pltpu.make_async_remote_copy(
                signal.at[:, pl.ds(cols - edge, edge)], sig.at[:, pl.ds(0, edge)],
                halo_send.at[0], halo_recv.at[0], device_id=right, device_id_type=MESH),
            pltpu.make_async_remote_copy(
                signal.at[:, pl.ds(0, edge)], sig.at[:, pl.ds(edge + cols, edge)],
                halo_send.at[1], halo_recv.at[1], device_id=left, device_id_type=MESH),
            pltpu.make_async_remote_copy(
                feat.at[:, pl.ds(cols, edge)], feat.at[:, pl.ds(0, edge)],
                halo_send.at[2], halo_recv.at[2], device_id=right, device_id_type=MESH),
            pltpu.make_async_remote_copy(
                feat.at[:, pl.ds(edge, edge)], feat.at[:, pl.ds(edge + cols, edge)],
                halo_send.at[3], halo_recv.at[3], device_id=left, device_id_type=MESH),
        ]

    def block_copy(i, slot):
        target = grp_peer(i)
        return pltpu.make_async_remote_copy(
            send_blocks.at[:, pl.ds(pl.multiple_of(target[1] * rslice, rslice), rslice), :],
            all_blocks.at[pl.ds(slot * mine, mine)],
            block_send.at[i], block_recv.at[i], device_id=target, device_id_type=MESH)

    def src_copy(i, slot):
        return pltpu.make_async_remote_copy(
            send_src, all_src.at[slot], src_send.at[i], src_recv.at[i],
            device_id=grp_peer(i), device_id_type=MESH)

    def reduce_copy(i, slot):
        target = grp_peer(i)
        return pltpu.make_async_remote_copy(
            part_t.at[pl.ds(pl.multiple_of(target[1] * rslice, rslice), rslice), :],
            reduce_in.at[slot], reduce_send.at[i], reduce_recv.at[i],
            device_id=target, device_id_type=MESH)

    def low_copy(i, slot):
        return pltpu.make_async_remote_copy(
            up.at[leaf], up.at[slot], low_send.at[i], low_recv.at[i],
            device_id=low_peer(i), device_id_type=MESH)

    def high_copy(i, slot):
        return pltpu.make_async_remote_copy(
            up.at[pl.ds(my_high * low, low)], up.at[pl.ds(slot * low, low)],
            high_send.at[i], high_recv.at[i], device_id=high_peer(i), device_id_type=MESH)

    def fred_copy(i, slot):
        target = grp_peer(i)
        return pltpu.make_async_remote_copy(
            part.at[pl.ds(pl.multiple_of(target[1] * vslice, vslice), vslice), :],
            field_in.at[slot], fred_send.at[i], fred_recv.at[i],
            device_id=target, device_id_type=MESH)

    def fgat_copy(i, slot):
        return pltpu.make_async_remote_copy(
            field.at[grp], field.at[slot], fgat_send.at[i], fgat_recv.at[i],
            device_id=grp_peer(i), device_id_type=MESH)

    def ring_copy(side, step, slot):
        target = grp_peer(1) if side == 0 else grp_peer(n_grp - 1)
        ref = coefs.at[slot]
        if step == half - 1:
            ref = ref.at[pl.ds(side * (leaves // 2), leaves // 2)]
        return pltpu.make_async_remote_copy(
            ref, ref, ring_send.at[side, step], ring_recv.at[side, step],
            device_id=target, device_id_type=MESH)

    def ring_start(step):
        ring_copy(0, step, lax.rem(grp + n_grp - step, n_grp)).start()
        ring_copy(1, step, lax.rem(grp + step, n_grp)).start()

    def ring_arrive(step):
        ring_copy(0, step, lax.rem(grp + n_grp - step - 1, n_grp)).wait_recv()
        ring_copy(1, step, lax.rem(grp + step + 1, n_grp)).wait_recv()

    for copy in halo_copies():
        copy.start()
    each(n_grp, lambda i: block_copy(i, grp).start())
    each(n_grp, lambda i: src_copy(i, grp).start())
    all_blocks[pl.ds(grp * mine, mine)] = send_blocks[
        :, pl.ds(pl.multiple_of(grp * rslice, rslice), rslice), :]

    loads[0].wait()
    loads[1].wait()

    def one_coef(l, carry):
        first = pl.multiple_of(edge + l * width, width)
        coefs[grp, l] = dot(sig[:, pl.ds(first, width)], base[l]).astype(BF)
        return carry

    lax.fori_loop(0, leaves, one_coef, 0, unroll=2)
    ring_start(0)
    loads[3].wait()
    upward = jnp.zeros((rows, rank), F32)
    for l in range(leaves):
        upward = upward + dot(coefs[grp, l], trans[l])
    part_t[...] = upward.T.astype(BF)
    each(n_grp, lambda i: reduce_copy(i, grp).start())
    reduce_in[grp] = part_t[pl.ds(pl.multiple_of(grp * rslice, rslice), rslice), :]

    def near(a, carry):
        here = pl.multiple_of(a * width, width)
        inner = pl.multiple_of((a - 2) * width, width)
        square = dot(feat_t[pl.ds(inner, width), :], feat[:, pl.ds(here, 3 * width)])
        close = lax.rsqrt(square).astype(BF)
        acc[:, pl.ds(here, 3 * width)] += dot(sig[:, pl.ds(here, width)], close)
        acc[:, pl.ds(here, width)] += dot(
            sig[:, pl.ds(here + width, 2 * width)], close[:, width:], ((1,), (1,)))
        return carry

    lax.fori_loop(2, 4, near, 0)

    each(n_grp, lambda i: reduce_copy(i, grp_from(i)).wait_recv())
    up[leaf] = jnp.sum(reduce_in[...].astype(F32), axis=0).astype(BF)
    each(low, lambda i: low_copy(i, leaf).start())
    ring_arrive(0)
    ring_start(1)

    lax.fori_loop(4, 6, near, 0)

    each(low, lambda i: low_copy(i, low_from(i)).wait_recv())
    each(high, lambda i: high_copy(i, my_high).start())
    each(n_grp, lambda i: src_copy(i, grp_from(i)).wait_recv())
    to_smem = pltpu.make_async_copy(all_src, src_smem, smem_sem)
    to_smem.start()
    if half > 2:
        ring_arrive(1)
        ring_start(2)

    lax.fori_loop(6, 8, near, 0)

    to_smem.wait()
    each(n_grp, lambda i: block_copy(i, grp_from(i)).wait_recv())
    each(high, lambda i: high_copy(i, high_from(i)).wait_recv())
    picked = jnp.concatenate(
        [up[src_smem[k // mine, k % mine, 0]] for k in range(mine * n_grp)], axis=0)
    stacked = jnp.concatenate([all_blocks[k] for k in range(mine * n_grp)], axis=0)
    part[...] = dot(picked, stacked, ((0,), (0,)))
    each(n_grp, lambda i: fred_copy(i, grp).start())
    field_in[grp] = part[pl.ds(pl.multiple_of(grp * vslice, vslice), vslice), :]
    if half > 3:
        ring_arrive(2)
        ring_start(3)

    for copy in halo_copies():
        copy.wait_recv()

    @pl.when(rank_id == 0)
    def _():
        sig[:, 0:edge] = jnp.zeros((rows, edge), BF)

    @pl.when(rank_id == total - 1)
    def _():
        sig[:, edge + cols :] = jnp.zeros((rows, edge), BF)

    lax.fori_loop(8, 2 + leaves, near, 0)

    each(n_grp, lambda i: fred_copy(i, grp_from(i)).wait_recv())
    field[grp] = jnp.sum(field_in[...], axis=0)
    each(n_grp, lambda i: fgat_copy(i, grp).start())

    square = dot(feat_t[0 : 2 * width, :], feat[:, 0:edge])
    close = lax.rsqrt(square).astype(BF)
    acc[:, edge : edge + width] += dot(sig[:, 0:edge], close[:width], ((1,), (1,)))
    acc[:, edge + width : edge + 2 * width] += dot(
        sig[:, width:edge], close[width:, width:], ((1,), (1,)))

    loads[4].wait()
    ring_arrive(half - 1)

    each(n_grp, lambda i: fgat_copy(i, grp_from(i)).wait_recv())
    top = field[...].reshape(rows, rank).astype(BF)
    scale = 0.5 / math.sqrt(extent)

    def finish(l, carry):
        tiles = []
        for k in range(slots):
            src = leaf_src[l, k]
            tile = coefs[src // leaves, lax.rem(src, leaves)]
            tiles.append(jnp.where(k < leaf_count[l], tile, jnp.zeros_like(tile)))
        weights = blocks[l].reshape(slots * rank, rank)
        total_field = dot(jnp.concatenate(tiles, axis=1), weights)
        total_field = (total_field + dot(top, trans[l], ((1,), (1,)))).astype(BF)
        first = pl.multiple_of(l * width, width)
        near_part = acc[:, pl.ds(pl.multiple_of(edge + l * width, width), width)]
        far_part = dot(total_field, base[l], ((1,), (1,)))
        result[:, pl.ds(first, width)] = (near_part * scale + far_part).astype(BF)
        return carry

    lax.fori_loop(0, leaves, finish, 0)
    store = pltpu.make_async_copy(result, out, store_sem)
    store.start()

    for copy in halo_copies():
        copy.wait_send()
    for step in range(half):
        ring_copy(0, step, lax.rem(grp + n_grp - step, n_grp)).wait_send()
        ring_copy(1, step, lax.rem(grp + step, n_grp)).wait_send()

    def drain(i):
        block_copy(i, grp).wait_send()
        src_copy(i, grp).wait_send()
        reduce_copy(i, grp).wait_send()
        fred_copy(i, grp).wait_send()
        fgat_copy(i, grp).wait_send()

    each(n_grp, drain)
    each(low, lambda i: low_copy(i, leaf).wait_send())
    each(high, lambda i: high_copy(i, my_high).wait_send())
    store.wait()


def shards(n_leaf, n_grp, low, signal, points, basis, transfer, leaf_src, leaf_count,
           leaf_blocks, cluster_src, cluster_count, cluster_blocks):
    rows, cols = signal.shape
    leaves, width, rank = basis.shape
    mine = cluster_blocks.shape[1]
    slots = leaf_blocks.shape[1]
    rslice = rank // n_grp
    vslice = rows // n_grp
    high = n_leaf // low
    half = n_grp // 2
    ext = cols + 4 * width
    dma = pltpu.SemaphoreType.DMA
    anywhere = pl.BlockSpec(memory_space=pl.ANY)
    vmem = pl.BlockSpec(memory_space=pltpu.VMEM)
    smem = pl.BlockSpec(memory_space=pltpu.SMEM)
    return pl.pallas_call(
        functools.partial(kernel, n_leaf, n_grp, low),
        out_shape=jax.ShapeDtypeStruct((rows, cols), BF),
        in_specs=[anywhere, vmem, anywhere, anywhere, smem, smem, anywhere, smem, smem, anywhere],
        out_specs=anywhere,
        scratch_shapes=[
            pltpu.VMEM((rows, ext), BF),
            pltpu.VMEM((16, ext), BF),
            pltpu.VMEM((cols, 16), BF),
            pltpu.VMEM((leaves, width, rank), BF),
            pltpu.VMEM((leaves, rank, rank), BF),
            pltpu.VMEM((leaves, slots, rank, rank), BF),
            pltpu.VMEM((n_grp, leaves, rows, rank), BF),
            pltpu.VMEM((rows, ext), F32),
            pltpu.VMEM((rows, cols), BF),
            pltpu.VMEM((rank, rows), BF),
            pltpu.VMEM((n_grp, rslice, rows), BF),
            pltpu.VMEM((n_leaf, rslice, rows), BF),
            pltpu.VMEM((mine, rank, rank), BF),
            pltpu.VMEM((mine, rank, rank), BF),
            pltpu.VMEM((mine * n_grp, rslice, rank), BF),
            pltpu.VMEM((8, 128), jnp.int32),
            pltpu.VMEM((n_grp, 8, 128), jnp.int32),
            pltpu.SMEM((n_grp, 8, 128), jnp.int32),
            pltpu.VMEM((rows, rank), F32),
            pltpu.VMEM((n_grp, vslice, rank), F32),
            pltpu.VMEM((n_grp, vslice, rank), F32),
            dma((5,)),
            dma((4,)), dma((4,)),
            dma((2, half)), dma((2, half)),
            dma((n_grp,)), dma((n_grp,)),
            dma((n_grp,)), dma((n_grp,)),
            dma((n_grp,)), dma((n_grp,)),
            dma((low,)), dma((low,)),
            dma((high,)), dma((high,)),
            dma((n_grp,)), dma((n_grp,)),
            dma((n_grp,)), dma((n_grp,)),
            dma, dma,
        ],
        compiler_params=pltpu.CompilerParams(
            collective_id=0, has_side_effects=True, vmem_limit_bytes=48 * 1024 * 1024),
        cost_estimate=pl.CostEstimate(
            flops=2 * rows * cols * 6 * width, bytes_accessed=6 * 1024 * 1024,
            transcendentals=3 * cols * width),
        name="h2_product",
    )(signal, points, basis, transfer, leaf_src, leaf_count, leaf_blocks,
      cluster_src, cluster_count, cluster_blocks[0])


def solution(mesh):
    both = ("leaf", "grp")
    placed = (
        P(None, both),
        P(None, both),
        P(both, None, None),
        P(both, None, None),
        P(both, None),
        P(both),
        P(both, None, None, None),
        P("leaf", "grp"),
        P("leaf"),
        P("leaf", "grp", None, None),
    )
    n_leaf, n_grp = mesh.shape["leaf"], mesh.shape["grp"]
    low = LOW if n_leaf > LOW else n_leaf // 2
    return jax.shard_map(
        functools.partial(shards, n_leaf, n_grp, low),
        mesh=mesh, in_specs=placed, out_specs=P(None, both), check_vma=False)
```

```python
import functools
import math

import jax
import jax.numpy as jnp
from jax import lax
from jax.experimental import pallas as pl
from jax.experimental.pallas import tpu as pltpu
from jax.sharding import PartitionSpec as P

BF = jnp.bfloat16
F32 = jnp.float32
MESH = pl.DeviceIdType.MESH
SOFTENING = 0.0025


def split3(value):
    first = value.astype(BF).astype(F32)
    rest = value - first
    second = rest.astype(BF).astype(F32)
    return first, second, rest - second


def dot(a, b, contract=((1,), (0,))):
    return lax.dot_general(a, b, (contract, ((), ())), preferred_element_type=F32)
VMEM_LIMIT = 63 * 1024 * 1024


def kernel(
    n_leaf, n_grp, n_x,
    signal, points, basis, transfer, leaf_src, leaf_count, leaf_blocks,
    cluster_src, cluster_count, cluster_blocks,
    out,
    sig, pts_in, feat, feat_t, base, trans, blocks, coefs, acc,
    part_t, reduce_in, pair, up, own_blocks, send_blocks, all_blocks,
    all_src, src_smem, field_in, across,
    load_sem, halo_send, halo_recv, ring_send, ring_recv,
    block_send, block_recv, src_send, src_recv, reduce_send, reduce_recv,
    pair_send, pair_recv, plane_send, plane_recv, field_send, field_recv, smem_sem,
):
    leaf = lax.axis_index("leaf")
    grp = lax.axis_index("grp")
    rows, cols = signal.shape
    leaves, width, rank = basis.shape
    slots = leaf_blocks.shape[1]
    mine = cluster_blocks.shape[0]
    rslice = rank // n_grp
    half = n_grp // 2
    n_y = n_leaf // (2 * n_x)
    chips = n_x * n_y
    edge = 2 * width
    extent = 5 * width
    core = lax.rem(leaf, 2)
    chip_y = lax.rem(leaf // 2, n_y)
    chip_x = leaf // (2 * n_y)
    rank_id = leaf * n_grp + grp
    total = n_leaf * n_grp
    right_id = lax.rem(rank_id + 1, total)
    left_id = lax.rem(rank_id + total - 1, total)
    right = (right_id // n_grp, lax.rem(right_id, n_grp))
    left = (left_id // n_grp, lax.rem(left_id, n_grp))
    other = (leaf + 1 - 2 * core, grp)

    def grp_peer(i):
        return (leaf, lax.rem(grp + i, n_grp))

    def plane_peer(i):
        to_x = lax.rem(chip_x + i // n_y, n_x)
        to_y = lax.rem(chip_y + lax.rem(i, n_y), n_y)
        return ((to_x * n_y + to_y) * 2 + core, grp)

    def each(n, fn):
        def body(i, carry):
            fn(i)
            return carry

        lax.fori_loop(1, n, body, 0)

    def remote(src, dst, send, recv, device):
        return pltpu.make_async_remote_copy(
            src, dst, send, recv, device_id=device, device_id_type=MESH)

    def wait_all(ref, n, sem):
        whole = ref.at[pl.ds(1, n - 1)]
        pltpu.make_async_copy(whole, whole, sem).wait()

    loads = [
        pltpu.make_async_copy(signal, sig.at[:, pl.ds(edge, cols)], load_sem.at[0]),
        pltpu.make_async_copy(basis, base, load_sem.at[1]),
        pltpu.make_async_copy(transfer, trans, load_sem.at[2]),
        pltpu.make_async_copy(points, pts_in, load_sem.at[3]),
        pltpu.make_async_copy(cluster_blocks, own_blocks, load_sem.at[4]),
        pltpu.make_async_copy(leaf_blocks, blocks, load_sem.at[5]),
    ]
    for load in loads[:5]:
        load.start()

    barrier = pltpu.get_barrier_semaphore()

    def greet(device):
        pl.semaphore_signal(barrier, inc=1, device_id=device, device_id_type=MESH)

    each(n_grp, lambda i: greet(grp_peer(i)))
    greet(other)
    greet(left)
    greet(right)
    each(chips, lambda i: greet(plane_peer(i)))

    def halo_copy(i):
        return [
            lambda: remote(signal.at[:, pl.ds(cols - edge, edge)], sig.at[:, pl.ds(0, edge)],
                           halo_send.at[0], halo_recv.at[0], right),
            lambda: remote(signal.at[:, pl.ds(0, edge)], sig.at[:, pl.ds(edge + cols, edge)],
                           halo_send.at[1], halo_recv.at[1], left),
            lambda: remote(feat.at[:, pl.ds(cols, edge)], feat.at[:, pl.ds(0, edge)],
                           halo_send.at[2], halo_recv.at[2], right),
            lambda: remote(feat.at[:, pl.ds(edge, edge)], feat.at[:, pl.ds(edge + cols, edge)],
                           halo_send.at[3], halo_recv.at[3], left),
        ][i]()

    def block_copy(i):
        target = grp_peer(i)
        return remote(
            send_blocks.at[:, pl.ds(pl.multiple_of(target[1] * rslice, rslice), rslice), :],
            all_blocks.at[i], block_send, block_recv, target)

    def src_copy(i):
        return remote(all_src.at[0], all_src.at[i], src_send, src_recv, grp_peer(i))

    def reduce_copy(i):
        target = grp_peer(i)
        return remote(
            part_t.at[pl.ds(pl.multiple_of(target[1] * rslice, rslice), rslice), :],
            reduce_in.at[i], reduce_send, reduce_recv, target)

    def pair_copy():
        return remote(pair.at[0], pair.at[1], pair_send, pair_recv, other)

    def plane_copy(i):
        return remote(up.at[0], up.at[i], plane_send, plane_recv, plane_peer(i))

    def field_copy(i):
        return remote(field_in.at[0], field_in.at[i], field_send, field_recv, grp_peer(i))

    def ring_copy(side, step, chunk, slot):
        target = grp_peer(1) if side == 0 else grp_peer(n_grp - 1)
        ref = coefs.at[slot, pl.ds(chunk * (leaves // 2), leaves // 2)]
        return remote(ref, ref, ring_send.at[side, step, chunk],
                      ring_recv.at[side, step, chunk], target)

    def ring_sides(step, chunk):
        return (0, 1) if step < half - 1 else (chunk,)

    def ring_start(step, chunk):
        for side in ring_sides(step, chunk):
            away = n_grp - step if side == 0 else step
            ring_copy(side, step, chunk, lax.rem(grp + away, n_grp)).start()

    def ring_arrive(step, chunk):
        for side in ring_sides(step, chunk):
            away = n_grp - step - 1 if side == 0 else step + 1
            ring_copy(side, step, chunk, lax.rem(grp + away, n_grp)).wait_recv()

    def ring_sent(step, chunk):
        for side in ring_sides(step, chunk):
            away = n_grp - step if side == 0 else step
            ring_copy(side, step, chunk, lax.rem(grp + away, n_grp)).wait_send()

    def ring_pass(step, chunk):
        if step < half:
            ring_arrive(step - 1, chunk)
            ring_start(step, chunk)

    pl.semaphore_wait(barrier, n_grp - 1 + chips - 1 + 3)
    halo_copy(0).start()
    halo_copy(1).start()

    loads[0].wait()
    loads[1].wait()
    for chunk in range(2):
        for l in range(chunk * leaves // 2, (chunk + 1) * leaves // 2):
            first = edge + l * width
            coefs[grp, l] = dot(sig[:, first : first + width], base[l]).astype(BF)
        ring_start(0, chunk)
    loads[2].wait()
    upward = jnp.zeros((rows, rank), F32)
    for l in range(leaves):
        upward = upward + dot(coefs[grp, l], trans[l])
    part_t[...] = upward.T.astype(BF)
    each(n_grp, lambda i: reduce_copy(i).start())
    reduce_in[0] = part_t[pl.ds(pl.multiple_of(grp * rslice, rslice), rslice), :]
    loads[5].start()

    loads[3].wait()
    pts = pts_in[...].astype(F32)
    norm = pts[0:1] * pts[0:1] + pts[1:2] * pts[1:2] + pts[2:3] * pts[2:3]
    pieces = jnp.concatenate(split3(norm), axis=0)
    ones = jnp.ones((3, cols), F32)
    soft = jnp.concatenate(split3(jnp.full((1, cols), SOFTENING, F32)), axis=0)
    fill = jnp.zeros((4, cols), F32)
    feat[:, edge : edge + cols] = jnp.concatenate(
        [-2.0 * pts, ones, pieces, ones, fill], axis=0).astype(BF)
    halo_copy(2).start()
    halo_copy(3).start()
    feat_t[...] = jnp.concatenate([pts, pieces, ones, soft, fill], axis=0).T.astype(BF)

    src_row = lax.broadcasted_iota(jnp.int32, (8, 128), 0)
    packed_src = jnp.zeros((8, 128), jnp.int32)
    for i in range(mine):
        packed_src = jnp.where(src_row == i, cluster_src[0, i], packed_src)
    all_src[0] = packed_src
    each(n_grp, lambda i: src_copy(i).start())
    loads[4].wait()
    for i in range(mine):
        alive = (grp * mine + i) < cluster_count[0]
        keep = jnp.where(alive, 1.0, 0.0)
        send_blocks[i] = (own_blocks[i].astype(F32) * keep).astype(BF)
    each(n_grp, lambda i: block_copy(i).start())
    all_blocks[0] = send_blocks[:, pl.ds(pl.multiple_of(grp * rslice, rslice), rslice), :]
    acc[...] = jnp.zeros_like(acc)

    def near(a):
        here = pl.multiple_of(a * width, width)
        inner = pl.multiple_of((a - 2) * width, width)
        square = dot(feat_t[pl.ds(inner, width), :], feat[:, pl.ds(here, 3 * width)])
        close = lax.rsqrt(square).astype(BF)
        acc[:, pl.ds(here, 3 * width)] += dot(sig[:, pl.ds(here, width)], close)
        acc[:, pl.ds(here, width)] += dot(
            sig[:, pl.ds(here + width, 2 * width)], close[:, width:], ((1,), (1,)))

    def slice_sum():
        wait_all(reduce_in, n_grp, reduce_recv)
        pair[0] = jnp.sum(reduce_in[...].astype(F32), axis=0).astype(BF)
        pair_copy().start()

    def plane_out():
        pair_copy().wait_recv()
        one, two = pair[0].astype(F32), pair[1].astype(F32)
        low = jnp.where(core == 0, one, two)
        high = jnp.where(core == 0, two, one)
        up[0] = jnp.concatenate([low, high], axis=1).astype(BF)
        each(chips, lambda i: plane_copy(i).start())

    def to_smem():
        return pltpu.make_async_copy(all_src, src_smem, smem_sem)

    def fetch_src():
        wait_all(all_src, n_grp, src_recv)
        to_smem().start()

    def couple():
        to_smem().wait()
        wait_all(all_blocks, n_grp, block_recv)
        wait_all(up, chips, plane_recv)
        tiles = []
        for i in range(n_grp):
            for j in range(mine):
                src = src_smem[i, j, 0]
                from_x = lax.rem(chip_x + n_x - src // (2 * n_y), n_x)
                from_y = lax.rem(chip_y + n_y - lax.rem(src // 2, n_y), n_y)
                tile = up[from_x * n_y + from_y]
                upper = lax.rem(src, 2) == 0
                tiles.append(jnp.where(upper, tile[:, :rows], tile[:, rows:]))
        stacked = jnp.concatenate(
            [all_blocks[i, j] for i in range(n_grp) for j in range(mine)], axis=0)
        field_in[0] = dot(jnp.concatenate(tiles, axis=0), stacked, ((0,), (0,))).astype(BF)
        each(n_grp, lambda i: field_copy(i).start())

    def halo_arrive():
        for i in range(4):
            halo_copy(i).wait_recv()

        @pl.when(rank_id == 0)
        def _():
            sig[:, 0:edge] = jnp.zeros((rows, edge), BF)

        @pl.when(rank_id == total - 1)
        def _():
            sig[:, edge + cols :] = jnp.zeros((rows, edge), BF)

    def events(a):
        if a == 2:
            ring_pass(1, 0)
        if a == 3:
            slice_sum()
            ring_pass(1, 1)
        if a == 4:
            plane_out()
            fetch_src()
        if a == 5:
            ring_pass(2, 0)
        if a == 6:
            ring_pass(2, 1)
        if a == 7:
            halo_arrive()
            ring_pass(3, 0)
        if a == 8:
            ring_pass(3, 1)

    def near_step(a, carry):
        near(a)
        for at in range(2, 9):
            @pl.when(a == at)
            def _():
                events(at)
        return carry

    lax.fori_loop(2, 2 + leaves, near_step, 0)
    couple()
    square = dot(feat_t[0 : 2 * width, :], feat[:, 0:edge])
    close = lax.rsqrt(square).astype(BF)
    acc[:, edge : edge + width] += dot(sig[:, 0:edge], close[:width], ((1,), (1,)))
    acc[:, edge + width : edge + 2 * width] += dot(
        sig[:, width:edge], close[width:, width:], ((1,), (1,)))

    loads[5].wait()
    ring_arrive(half - 1, 0)
    ring_arrive(half - 1, 1)
    for l in range(leaves):
        tiles = []
        for k in range(slots):
            src = leaf_src[l, k]
            tile = coefs[src // leaves, lax.rem(src, leaves)]
            tiles.append(jnp.where(k < leaf_count[l], tile, jnp.zeros_like(tile)))
        weights = blocks[l].reshape(slots * rank, rank)
        across[l] = dot(jnp.concatenate(tiles, axis=1), weights)

    wait_all(field_in, n_grp, field_recv)
    top = jnp.sum(field_in[...].astype(F32), axis=0).astype(BF)
    scale = 0.5 / math.sqrt(extent)
    for l in range(leaves):
        leaf_field = (across[l] + dot(top, trans[l], ((1,), (1,)))).astype(BF)
        near_part = acc[:, edge + l * width : edge + (l + 1) * width]
        far_part = dot(leaf_field, base[l], ((1,), (1,)))
        out[:, l * width : (l + 1) * width] = (near_part * scale + far_part).astype(BF)

    for i in range(4):
        halo_copy(i).wait_send()
    for step in range(half):
        for chunk in range(2):
            ring_sent(step, chunk)
    wait_all(all_blocks, n_grp, block_send)
    wait_all(all_src, n_grp, src_send)
    wait_all(reduce_in, n_grp, reduce_send)
    pair_copy().wait_send()
    wait_all(up, chips, plane_send)
    wait_all(field_in, n_grp, field_send)


def shards(n_leaf, n_grp, n_x, signal, points, basis, transfer, leaf_src, leaf_count,
           leaf_blocks, cluster_src, cluster_count, cluster_blocks):
    rows, cols = signal.shape
    leaves, width, rank = basis.shape
    mine = cluster_blocks.shape[1]
    slots = leaf_blocks.shape[1]
    rslice = rank // n_grp
    half = n_grp // 2
    ext = cols + 4 * width
    dma = pltpu.SemaphoreType.DMA
    hbm = pl.BlockSpec(memory_space=pltpu.HBM)
    vmem = pl.BlockSpec(memory_space=pltpu.VMEM)
    smem = pl.BlockSpec(memory_space=pltpu.SMEM)
    return pl.pallas_call(
        functools.partial(kernel, n_leaf, n_grp, n_x),
        out_shape=jax.ShapeDtypeStruct((rows, cols), BF),
        in_specs=[hbm, hbm, hbm, hbm, smem, smem, hbm, smem, smem, hbm],
        out_specs=vmem,
        scratch_shapes=[
            pltpu.VMEM((rows, ext), BF),
            pltpu.VMEM(points.shape, BF),
            pltpu.VMEM((16, ext), BF),
            pltpu.VMEM((cols, 16), BF),
            pltpu.VMEM((leaves, width, rank), BF),
            pltpu.VMEM((leaves, rank, rank), BF),
            pltpu.VMEM((leaves, slots, rank, rank), BF),
            pltpu.VMEM((n_grp, leaves, rows, rank), BF),
            pltpu.VMEM((rows, ext), F32),
            pltpu.VMEM((rank, rows), BF),
            pltpu.VMEM((n_grp, rslice, rows), BF),
            pltpu.VMEM((2, rslice, rows), BF),
            pltpu.VMEM((n_leaf // 2, rslice, 2 * rows), BF),
            pltpu.VMEM((mine, rank, rank), BF),
            pltpu.VMEM((mine, rank, rank), BF),
            pltpu.VMEM((n_grp, mine, rslice, rank), BF),
            pltpu.VMEM((n_grp, 8, 128), jnp.int32),
            pltpu.SMEM((n_grp, 8, 128), jnp.int32),
            pltpu.VMEM((n_grp, rows, rank), BF),
            pltpu.VMEM((leaves, rows, rank), F32),
            dma((6,)),
            dma((4,)), dma((4,)),
            dma((2, half, 2)), dma((2, half, 2)),
            dma, dma, dma, dma, dma, dma, dma, dma, dma, dma, dma, dma, dma,
        ],
        compiler_params=pltpu.CompilerParams(
            collective_id=0, has_side_effects=True, vmem_limit_bytes=VMEM_LIMIT),
        cost_estimate=pl.CostEstimate(
            flops=2 * rows * cols * 6 * width, bytes_accessed=6 * 1024 * 1024,
            transcendentals=3 * cols * width),
        name="h2_product",
    )(signal, points, basis, transfer, leaf_src, leaf_count, leaf_blocks,
      cluster_src, cluster_count, cluster_blocks[0])


def solution(mesh):
    both = ("leaf", "grp")
    placed = (
        P(None, both),
        P(None, both),
        P(both, None, None),
        P(both, None, None),
        P(both, None),
        P(both),
        P(both, None, None, None),
        P("leaf", "grp"),
        P("leaf"),
        P("leaf", "grp", None, None),
    )
    n_leaf, n_grp = mesh.shape["leaf"], mesh.shape["grp"]
    n_x = 4 if n_leaf == 64 else 2
    return jax.shard_map(
        functools.partial(shards, n_leaf, n_grp, n_x),
        mesh=mesh, in_specs=placed, out_specs=P(None, both), check_vma=False)
```

```python
import functools
import math

import jax
import jax.numpy as jnp
from jax import lax
from jax.experimental import pallas as pl
from jax.experimental.pallas import tpu as pltpu
from jax.sharding import PartitionSpec as P

BF = jnp.bfloat16
F32 = jnp.float32
MESH = pl.DeviceIdType.MESH
SOFTENING = 0.0025


def split3(value):
    first = value.astype(BF).astype(F32)
    rest = value - first
    second = rest.astype(BF).astype(F32)
    return first, second, rest - second


def dot(a, b, contract=((1,), (0,))):
    return lax.dot_general(a, b, (contract, ((), ())), preferred_element_type=F32)
VMEM_LIMIT = 48 * 1024 * 1024


def kernel(
    n_leaf, n_grp, n_x,
    signal, points, basis, transfer, leaf_src_in, leaf_count_in, leaf_blocks,
    cluster_src_in, cluster_count, cluster_blocks,
    out,
    leaf_src, leaf_count, cluster_src,
    sig, pts_in, feat, feat_t, base, trans, blocks, coefs, acc,
    part_t, reduce_in, pair, up, own_blocks, send_blocks, all_blocks,
    all_src, src_smem, field_in, across,
    load_sem, halo_send, halo_recv, ring_send, ring_recv,
    block_send, block_recv, src_send, src_recv, reduce_send, reduce_recv,
    pair_send, pair_recv, plane_send, plane_recv, field_send, field_recv, smem_sem,
):
    leaf = lax.axis_index("leaf")
    grp = lax.axis_index("grp")
    rows, cols = signal.shape
    leaves, width, rank = basis.shape
    slots = leaf_blocks.shape[1]
    mine = cluster_blocks.shape[0]
    rslice = rank // n_grp
    half = n_grp // 2
    n_y = n_leaf // (2 * n_x)
    chips = n_x * n_y
    edge = 2 * width
    extent = 5 * width
    core = lax.rem(leaf, 2)
    chip_y = lax.rem(leaf // 2, n_y)
    chip_x = leaf // (2 * n_y)
    rank_id = leaf * n_grp + grp
    total = n_leaf * n_grp
    right_id = lax.rem(rank_id + 1, total)
    left_id = lax.rem(rank_id + total - 1, total)
    right = (right_id // n_grp, lax.rem(right_id, n_grp))
    left = (left_id // n_grp, lax.rem(left_id, n_grp))
    other = (leaf + 1 - 2 * core, grp)

    def grp_peer(i):
        return (leaf, lax.rem(grp + i, n_grp))

    def plane_peer(i):
        to_x = lax.rem(chip_x + i // n_y, n_x)
        to_y = lax.rem(chip_y + lax.rem(i, n_y), n_y)
        return ((to_x * n_y + to_y) * 2 + core, grp)

    def ring_distance(i, n):
        return min(i % n, n - i % n)

    grp_order = sorted(range(1, n_grp), key=lambda i: -ring_distance(i, n_grp))
    plane_order = sorted(
        range(1, chips),
        key=lambda i: -ring_distance(i // n_y, n_x) - ring_distance(i % n_y, n_y))

    def each(order, fn):
        for i in order:
            fn(i)

    def remote(src, dst, send, recv, device):
        return pltpu.make_async_remote_copy(
            src, dst, send, recv, device_id=device, device_id_type=MESH)

    def wait_all(ref, n, sem):
        whole = ref.at[pl.ds(1, n - 1)]
        pltpu.make_async_copy(whole, whole, sem).wait()

    loads = [
        pltpu.make_async_copy(signal, sig.at[:, pl.ds(edge, cols)], load_sem.at[0]),
        pltpu.make_async_copy(basis, base, load_sem.at[1]),
        pltpu.make_async_copy(transfer, trans, load_sem.at[2]),
        pltpu.make_async_copy(points, pts_in, load_sem.at[3]),
        pltpu.make_async_copy(cluster_blocks, own_blocks, load_sem.at[4]),
        pltpu.make_async_copy(leaf_blocks, blocks, load_sem.at[5]),
        pltpu.make_async_copy(cluster_src_in, cluster_src, load_sem.at[6]),
        pltpu.make_async_copy(leaf_src_in, leaf_src, load_sem.at[8]),
        pltpu.make_async_copy(leaf_count_in, leaf_count, load_sem.at[9]),
    ]
    for load in loads[:5] + loads[6:]:
        load.start()

    barrier = pltpu.get_barrier_semaphore()

    def greet(device):
        pl.semaphore_signal(barrier, inc=1, device_id=device, device_id_type=MESH)

    each(plane_order, lambda i: greet(plane_peer(i)))
    each(grp_order, lambda i: greet(grp_peer(i)))
    greet(left)
    greet(right)
    greet(other)

    def halo_copy(i):
        return [
            lambda: remote(signal.at[:, pl.ds(cols - edge, edge)], sig.at[:, pl.ds(0, edge)],
                           halo_send.at[0], halo_recv.at[0], right),
            lambda: remote(signal.at[:, pl.ds(0, edge)], sig.at[:, pl.ds(edge + cols, edge)],
                           halo_send.at[1], halo_recv.at[1], left),
            lambda: remote(feat.at[:, pl.ds(cols, edge)], feat.at[:, pl.ds(0, edge)],
                           halo_send.at[2], halo_recv.at[2], right),
            lambda: remote(feat.at[:, pl.ds(edge, edge)], feat.at[:, pl.ds(edge + cols, edge)],
                           halo_send.at[3], halo_recv.at[3], left),
        ][i]()

    def block_copy(i):
        target = grp_peer(i)
        return remote(
            send_blocks.at[:, pl.ds(pl.multiple_of(target[1] * rslice, rslice), rslice), :],
            all_blocks.at[i], block_send, block_recv, target)

    def src_copy(i):
        return remote(all_src.at[0], all_src.at[i], src_send, src_recv, grp_peer(i))

    def reduce_copy(i):
        target = grp_peer(i)
        return remote(
            part_t.at[pl.ds(pl.multiple_of(target[1] * rslice, rslice), rslice), :],
            reduce_in.at[i], reduce_send, reduce_recv, target)

    def pair_copy():
        return remote(pair.at[0], pair.at[1], pair_send, pair_recv, other)

    def plane_copy(i):
        return remote(up.at[0], up.at[i], plane_send, plane_recv, plane_peer(i))

    def field_copy(i):
        return remote(field_in.at[0], field_in.at[i], field_send, field_recv, grp_peer(i))

    def ring_copy(side, step, chunk, slot):
        target = grp_peer(1) if side == 0 else grp_peer(n_grp - 1)
        ref = coefs.at[slot, pl.ds(chunk * (leaves // 2), leaves // 2)]
        return remote(ref, ref, ring_send.at[side, step, chunk],
                      ring_recv.at[side, step, chunk], target)

    def ring_sides(step, chunk):
        return (0, 1) if step < half - 1 else (chunk,)

    def ring_start(step, chunk):
        for side in ring_sides(step, chunk):
            away = n_grp - step if side == 0 else step
            ring_copy(side, step, chunk, lax.rem(grp + away, n_grp)).start()

    def ring_arrive(step, chunk):
        for side in ring_sides(step, chunk):
            away = n_grp - step - 1 if side == 0 else step + 1
            ring_copy(side, step, chunk, lax.rem(grp + away, n_grp)).wait_recv()

    def ring_sent(step, chunk):
        for side in ring_sides(step, chunk):
            away = n_grp - step if side == 0 else step
            ring_copy(side, step, chunk, lax.rem(grp + away, n_grp)).wait_send()

    def ring_pass(step, chunk):
        if step < half:
            ring_arrive(step - 1, chunk)
            ring_start(step, chunk)

    loads[0].wait()
    loads[1].wait()
    loads[5].start()
    for l in range(leaves):
        first = edge + l * width
        coefs[grp, l] = dot(sig[:, first : first + width], base[l]).astype(BF)
    loads[2].wait()
    upward = jnp.zeros((rows, rank), F32)
    for l in range(leaves):
        upward = upward + dot(coefs[grp, l], trans[l])
    part_t[...] = upward.T.astype(BF)
    pl.semaphore_wait(barrier, n_grp - 1 + chips - 1 + 3)
    each(grp_order, lambda i: reduce_copy(i).start())
    ring_start(0, 0)
    ring_start(0, 1)
    reduce_in[0] = part_t[pl.ds(pl.multiple_of(grp * rslice, rslice), rslice), :]

    loads[3].wait()
    pts = pts_in[...].astype(F32)
    norm = pts[0:1] * pts[0:1] + pts[1:2] * pts[1:2] + pts[2:3] * pts[2:3]
    pieces = jnp.concatenate(split3(norm), axis=0)
    ones = jnp.ones((3, cols), F32)
    soft = jnp.concatenate(split3(jnp.full((1, cols), SOFTENING, F32)), axis=0)
    fill = jnp.zeros((4, cols), F32)
    feat[:, edge : edge + cols] = jnp.concatenate(
        [-2.0 * pts, ones, pieces, ones, fill], axis=0).astype(BF)
    feat_t[...] = jnp.concatenate([pts, pieces, ones, soft, fill], axis=0).T.astype(BF)

    loads[6].wait()
    src_row = lax.broadcasted_iota(jnp.int32, (8, 128), 0)
    packed_src = jnp.zeros((8, 128), jnp.int32)
    for i in range(mine):
        packed_src = jnp.where(src_row == i, cluster_src[0, i], packed_src)
    all_src[0] = packed_src
    each(grp_order, lambda i: src_copy(i).start())
    loads[4].wait()
    for i in range(mine):
        alive = (grp * mine + i) < cluster_count[0]
        keep = jnp.where(alive, 1.0, 0.0)
        send_blocks[i] = (own_blocks[i].astype(F32) * keep).astype(BF)
    each(grp_order, lambda i: block_copy(i).start())
    all_blocks[0] = send_blocks[:, pl.ds(pl.multiple_of(grp * rslice, rslice), rslice), :]
    for i in range(4):
        halo_copy(i).start()
    acc[...] = jnp.zeros_like(acc)

    def near(a):
        here = pl.multiple_of(a * width, width)
        inner = pl.multiple_of((a - 2) * width, width)
        square = dot(feat_t[pl.ds(inner, width), :], feat[:, pl.ds(here, 3 * width)])
        close = lax.rsqrt(square).astype(BF)
        acc[:, pl.ds(here, 3 * width)] += dot(sig[:, pl.ds(here, width)], close)
        acc[:, pl.ds(here, width)] += dot(
            sig[:, pl.ds(here + width, 2 * width)], close[:, width:], ((1,), (1,)))

    def slice_sum():
        wait_all(reduce_in, n_grp, reduce_recv)
        pair[0] = jnp.sum(reduce_in[...].astype(F32), axis=0).astype(BF)
        pair_copy().start()

    def plane_out():
        pair_copy().wait_recv()
        one, two = pair[0].astype(F32), pair[1].astype(F32)
        low = jnp.where(core == 0, one, two)
        high = jnp.where(core == 0, two, one)
        up[0] = jnp.concatenate([low, high], axis=1).astype(BF)
        each(plane_order, lambda i: plane_copy(i).start())

    def to_smem():
        return pltpu.make_async_copy(all_src, src_smem, smem_sem)

    def fetch_src():
        wait_all(all_src, n_grp, src_recv)
        to_smem().start()

    def couple():
        to_smem().wait()
        wait_all(all_blocks, n_grp, block_recv)
        wait_all(up, chips, plane_recv)
        tiles = []
        for i in range(n_grp):
            for j in range(mine):
                src = src_smem[i, j, 0]
                from_x = lax.rem(chip_x + n_x - src // (2 * n_y), n_x)
                from_y = lax.rem(chip_y + n_y - lax.rem(src // 2, n_y), n_y)
                tile = up[from_x * n_y + from_y]
                upper = lax.rem(src, 2) == 0
                tiles.append(jnp.where(upper, tile[:, :rows], tile[:, rows:]))
        stacked = jnp.concatenate(
            [all_blocks[i, j] for i in range(n_grp) for j in range(mine)], axis=0)
        field_in[0] = dot(jnp.concatenate(tiles, axis=0), stacked, ((0,), (0,))).astype(BF)
        each(grp_order, lambda i: field_copy(i).start())

    def halo_arrive():
        for i in range(4):
            halo_copy(i).wait_recv()

        @pl.when(rank_id == 0)
        def _():
            sig[:, 0:edge] = jnp.zeros((rows, edge), BF)

        @pl.when(rank_id == total - 1)
        def _():
            sig[:, edge + cols :] = jnp.zeros((rows, edge), BF)

    def events(a):
        if a == 2:
            ring_pass(1, 0)
        if a == 3:
            slice_sum()
            ring_pass(1, 1)
        if a == 4:
            plane_out()
            fetch_src()
        if a == 5:
            ring_pass(2, 0)
        if a == 6:
            ring_pass(2, 1)
        if a == 7:
            halo_arrive()
            ring_pass(3, 0)
        if a == 8:
            ring_pass(3, 1)

    def near_step(a, carry):
        near(a)
        for at in range(2, 9):
            @pl.when(a == at)
            def _():
                events(at)
        return carry

    lax.fori_loop(2, 2 + leaves, near_step, 0)
    couple()
    square = dot(feat_t[0 : 2 * width, :], feat[:, 0:edge])
    close = lax.rsqrt(square).astype(BF)
    acc[:, edge : edge + width] += dot(sig[:, 0:edge], close[:width], ((1,), (1,)))
    acc[:, edge + width : edge + 2 * width] += dot(
        sig[:, width:edge], close[width:, width:], ((1,), (1,)))

    loads[5].wait()
    loads[7].wait()
    loads[8].wait()
    ring_arrive(half - 1, 0)
    ring_arrive(half - 1, 1)
    for l in range(leaves):
        tiles = []
        for k in range(slots):
            src = leaf_src[l, k]
            tile = coefs[src // leaves, lax.rem(src, leaves)]
            tiles.append(jnp.where(k < leaf_count[l], tile, jnp.zeros_like(tile)))
        weights = blocks[l].reshape(slots * rank, rank)
        across[l] = dot(jnp.concatenate(tiles, axis=1), weights)

    wait_all(field_in, n_grp, field_recv)
    top = jnp.sum(field_in[...].astype(F32), axis=0).astype(BF)
    scale = 0.5 / math.sqrt(extent)
    for l in range(leaves):
        leaf_field = (across[l] + dot(top, trans[l], ((1,), (1,)))).astype(BF)
        near_part = acc[:, edge + l * width : edge + (l + 1) * width]
        far_part = dot(leaf_field, base[l], ((1,), (1,)))
        out[:, l * width : (l + 1) * width] = (near_part * scale + far_part).astype(BF)

    for i in range(4):
        halo_copy(i).wait_send()
    for step in range(half):
        for chunk in range(2):
            ring_sent(step, chunk)
    wait_all(all_blocks, n_grp, block_send)
    wait_all(all_src, n_grp, src_send)
    wait_all(reduce_in, n_grp, reduce_send)
    pair_copy().wait_send()
    wait_all(up, chips, plane_send)
    wait_all(field_in, n_grp, field_send)


def shards(n_leaf, n_grp, n_x, signal, points, basis, transfer, leaf_src, leaf_count,
           leaf_blocks, cluster_src, cluster_count, cluster_blocks):
    rows, cols = signal.shape
    leaves, width, rank = basis.shape
    mine = cluster_blocks.shape[1]
    slots = leaf_blocks.shape[1]
    rslice = rank // n_grp
    half = n_grp // 2
    ext = cols + 4 * width
    dma = pltpu.SemaphoreType.DMA
    hbm = pl.BlockSpec(memory_space=pltpu.HBM)
    operands = [pltpu.with_memory_space_constraint(v, pltpu.HBM) for v in (
        signal, points, basis, transfer, leaf_src, leaf_count, leaf_blocks,
        cluster_src, cluster_blocks[0])]
    operands.insert(8, cluster_count)
    smem = pl.BlockSpec(memory_space=pltpu.SMEM)
    vmem = pl.BlockSpec(memory_space=pltpu.VMEM)
    return pl.pallas_call(
        functools.partial(kernel, n_leaf, n_grp, n_x),
        out_shape=jax.ShapeDtypeStruct((rows, cols), BF),
        in_specs=[hbm] * 8 + [smem, hbm],
        out_specs=vmem,
        scratch_shapes=[
            pltpu.SMEM(leaf_src.shape, jnp.int32),
            pltpu.SMEM(leaf_count.shape, jnp.int32),
            pltpu.SMEM(cluster_src.shape, jnp.int32),
            pltpu.VMEM((rows, ext), BF),
            pltpu.VMEM(points.shape, BF),
            pltpu.VMEM((16, ext), BF),
            pltpu.VMEM((cols, 16), BF),
            pltpu.VMEM((leaves, width, rank), BF),
            pltpu.VMEM((leaves, rank, rank), BF),
            pltpu.VMEM((leaves, slots, rank, rank), BF),
            pltpu.VMEM((n_grp, leaves, rows, rank), BF),
            pltpu.VMEM((rows, ext), F32),
            pltpu.VMEM((rank, rows), BF),
            pltpu.VMEM((n_grp, rslice, rows), BF),
            pltpu.VMEM((2, rslice, rows), BF),
            pltpu.VMEM((n_leaf // 2, rslice, 2 * rows), BF),
            pltpu.VMEM((mine, rank, rank), BF),
            pltpu.VMEM((mine, rank, rank), BF),
            pltpu.VMEM((n_grp, mine, rslice, rank), BF),
            pltpu.VMEM((n_grp, 8, 128), jnp.int32),
            pltpu.SMEM((n_grp, 8, 128), jnp.int32),
            pltpu.VMEM((n_grp, rows, rank), BF),
            pltpu.VMEM((leaves, rows, rank), F32),
            dma((10,)),
            dma((4,)), dma((4,)),
            dma((2, half, 2)), dma((2, half, 2)),
            dma, dma, dma, dma, dma, dma, dma, dma, dma, dma, dma, dma, dma,
        ],
        compiler_params=pltpu.CompilerParams(
            collective_id=0, has_side_effects=True, vmem_limit_bytes=VMEM_LIMIT),
        cost_estimate=pl.CostEstimate(
            flops=2 * rows * cols * 6 * width, bytes_accessed=6 * 1024 * 1024,
            transcendentals=3 * cols * width),
        name="h2_product",
    )(*operands)


def solution(mesh):
    both = ("leaf", "grp")
    placed = (
        P(None, both),
        P(None, both),
        P(both, None, None),
        P(both, None, None),
        P(both, None),
        P(both),
        P(both, None, None, None),
        P("leaf", "grp"),
        P("leaf"),
        P("leaf", "grp", None, None),
    )
    n_leaf, n_grp = mesh.shape["leaf"], mesh.shape["grp"]
    n_x = 4 if n_leaf == 64 else 2
    return jax.shard_map(
        functools.partial(shards, n_leaf, n_grp, n_x),
        mesh=mesh, in_specs=placed, out_specs=P(None, both), check_vma=False)
```

```python
import functools
import math

import jax
import jax.numpy as jnp
from jax import lax
from jax.experimental import pallas as pl
from jax.experimental.pallas import tpu as pltpu
from jax.sharding import PartitionSpec as P

BF = jnp.bfloat16
F32 = jnp.float32
MESH = pl.DeviceIdType.MESH
SOFTENING = 0.0025


def split3(value):
    first = value.astype(BF).astype(F32)
    rest = value - first
    second = rest.astype(BF).astype(F32)
    return first, second, rest - second


def dot(a, b, contract=((1,), (0,))):
    return lax.dot_general(a, b, (contract, ((), ())), preferred_element_type=F32)
VMEM_LIMIT = 48 * 1024 * 1024


def kernel(
    n_leaf, n_grp, n_x,
    signal, points, basis, transfer, leaf_src_in, leaf_count_in, leaf_blocks,
    cluster_src_in, cluster_count, cluster_blocks,
    out,
    leaf_src, leaf_count, cluster_src,
    sig, pts_in, pts_halo, feat, feat_t, base, trans, blocks, coefs, acc,
    part_t, reduce_in, pair, up, own_blocks, send_blocks, all_blocks,
    all_src, src_smem, field_in, down,
    load_sem, halo_send, halo_recv, ring_send, ring_recv,
    block_send, block_recv, src_send, src_recv, reduce_send, reduce_recv,
    pair_send, pair_recv, plane_send, plane_recv, field_send, field_recv, smem_sem,
):
    leaf = lax.axis_index("leaf")
    grp = lax.axis_index("grp")
    rows, cols = signal.shape
    leaves, width, rank = basis.shape
    slots = leaf_blocks.shape[1]
    mine = cluster_blocks.shape[0]
    rslice = rank // n_grp
    half = n_grp // 2
    n_y = n_leaf // (2 * n_x)
    chips = n_x * n_y
    edge = 2 * width
    extent = 5 * width
    core = lax.rem(leaf, 2)
    chip_y = lax.rem(leaf // 2, n_y)
    chip_x = leaf // (2 * n_y)
    rank_id = leaf * n_grp + grp
    total = n_leaf * n_grp
    right_id = lax.rem(rank_id + 1, total)
    left_id = lax.rem(rank_id + total - 1, total)
    right = (right_id // n_grp, lax.rem(right_id, n_grp))
    left = (left_id // n_grp, lax.rem(left_id, n_grp))
    other = (leaf + 1 - 2 * core, grp)

    def grp_peer(i):
        return (leaf, lax.rem(grp + i, n_grp))

    def plane_peer(i):
        to_x = lax.rem(chip_x + i // n_y, n_x)
        to_y = lax.rem(chip_y + lax.rem(i, n_y), n_y)
        return ((to_x * n_y + to_y) * 2 + core, grp)

    def ring_distance(i, n):
        return min(i % n, n - i % n)

    grp_order = sorted(range(1, n_grp), key=lambda i: -ring_distance(i, n_grp))
    plane_order = sorted(
        range(1, chips),
        key=lambda i: -ring_distance(i // n_y, n_x) - ring_distance(i % n_y, n_y))

    def each(order, fn):
        for i in order:
            fn(i)

    def remote(src, dst, send, recv, device):
        return pltpu.make_async_remote_copy(
            src, dst, send, recv, device_id=device, device_id_type=MESH)

    def wait_all(ref, n, sem):
        whole = ref.at[pl.ds(1, n - 1)]
        pltpu.make_async_copy(whole, whole, sem).wait()

    loads = [
        pltpu.make_async_copy(signal, sig.at[:, pl.ds(edge, cols)], load_sem.at[0]),
        pltpu.make_async_copy(basis, base, load_sem.at[1]),
        pltpu.make_async_copy(transfer, trans, load_sem.at[2]),
        pltpu.make_async_copy(points, pts_in, load_sem.at[3]),
        pltpu.make_async_copy(cluster_blocks, own_blocks, load_sem.at[4]),
        pltpu.make_async_copy(leaf_blocks, blocks, load_sem.at[5]),
        pltpu.make_async_copy(cluster_src_in, cluster_src, load_sem.at[6]),
        pltpu.make_async_copy(leaf_src_in, leaf_src, load_sem.at[8]),
        pltpu.make_async_copy(leaf_count_in, leaf_count, load_sem.at[9]),
    ]
    for load in loads[:5] + loads[6:]:
        load.start()

    barrier = pltpu.get_barrier_semaphore()

    def greet(device):
        pl.semaphore_signal(barrier, inc=1, device_id=device, device_id_type=MESH)

    each(plane_order, lambda i: greet(plane_peer(i)))
    each(grp_order, lambda i: greet(grp_peer(i)))
    greet(left)
    greet(right)
    greet(other)

    def halo_copy(i):
        return [
            lambda: remote(signal.at[:, pl.ds(cols - edge, edge)], sig.at[:, pl.ds(0, edge)],
                           halo_send.at[0], halo_recv.at[0], right),
            lambda: remote(signal.at[:, pl.ds(0, edge)], sig.at[:, pl.ds(edge + cols, edge)],
                           halo_send.at[1], halo_recv.at[1], left),
            lambda: remote(points.at[:, pl.ds(cols - edge, edge)], pts_halo.at[0],
                           halo_send.at[2], halo_recv.at[2], right),
            lambda: remote(points.at[:, pl.ds(0, edge)], pts_halo.at[1],
                           halo_send.at[3], halo_recv.at[3], left),
        ][i]()

    def block_copy(i):
        target = grp_peer(i)
        return remote(
            send_blocks.at[:, pl.ds(pl.multiple_of(target[1] * rslice, rslice), rslice), :],
            all_blocks.at[i], block_send, block_recv, target)

    def src_copy(i):
        return remote(all_src.at[0], all_src.at[i], src_send, src_recv, grp_peer(i))

    def reduce_copy(i):
        target = grp_peer(i)
        return remote(
            part_t.at[pl.ds(pl.multiple_of(target[1] * rslice, rslice), rslice), :],
            reduce_in.at[i], reduce_send, reduce_recv, target)

    def pair_copy():
        return remote(pair.at[0], pair.at[1], pair_send, pair_recv, other)

    def plane_copy(i):
        return remote(up.at[0], up.at[i], plane_send, plane_recv, plane_peer(i))

    def field_copy(i):
        return remote(field_in.at[0], field_in.at[i], field_send, field_recv, grp_peer(i))

    def ring_copy(side, step, chunk, slot):
        target = grp_peer(1) if side == 0 else grp_peer(n_grp - 1)
        ref = coefs.at[slot, pl.ds(chunk * (leaves // 2), leaves // 2)]
        return remote(ref, ref, ring_send.at[side, step, chunk],
                      ring_recv.at[side, step, chunk], target)

    def ring_sides(step, chunk):
        return (0, 1) if step < half - 1 else (chunk,)

    def ring_start(step, chunk):
        for side in ring_sides(step, chunk):
            away = n_grp - step if side == 0 else step
            ring_copy(side, step, chunk, lax.rem(grp + away, n_grp)).start()

    def ring_arrive(step, chunk):
        for side in ring_sides(step, chunk):
            away = n_grp - step - 1 if side == 0 else step + 1
            ring_copy(side, step, chunk, lax.rem(grp + away, n_grp)).wait_recv()

    def ring_sent(step, chunk):
        for side in ring_sides(step, chunk):
            away = n_grp - step if side == 0 else step
            ring_copy(side, step, chunk, lax.rem(grp + away, n_grp)).wait_send()

    def ring_pass(step, chunk):
        if step < half:
            ring_arrive(step - 1, chunk)
            ring_start(step, chunk)

    loads[0].wait()
    loads[1].wait()
    loads[5].start()
    for l in range(leaves):
        first = edge + l * width
        coefs[grp, l] = dot(sig[:, first : first + width], base[l]).astype(BF)
    loads[2].wait()
    upward = jnp.zeros((rows, rank), F32)
    for l in range(leaves):
        upward = upward + dot(coefs[grp, l], trans[l])
    part_t[...] = upward.T.astype(BF)
    pl.semaphore_wait(barrier, n_grp - 1 + chips - 1 + 3)
    each(grp_order, lambda i: reduce_copy(i).start())
    ring_start(0, 0)
    ring_start(0, 1)
    reduce_in[0] = part_t[pl.ds(pl.multiple_of(grp * rslice, rslice), rslice), :]

    def features(cells):
        pts = cells.astype(F32)
        n = pts.shape[1]
        norm = pts[0:1] * pts[0:1] + pts[1:2] * pts[1:2] + pts[2:3] * pts[2:3]
        pieces = jnp.concatenate(split3(norm), axis=0)
        ones = jnp.ones((3, n), F32)
        soft = jnp.concatenate(split3(jnp.full((1, n), SOFTENING, F32)), axis=0)
        fill = jnp.zeros((4, n), F32)
        one = jnp.concatenate([-2.0 * pts, ones, pieces, ones, fill], axis=0).astype(BF)
        return one, jnp.concatenate([pts, pieces, ones, soft, fill], axis=0)

    loads[3].wait()
    here_feat, here_other = features(pts_in[...])
    feat[:, edge : edge + cols] = here_feat
    feat_t[...] = here_other.T.astype(BF)

    loads[6].wait()
    src_lane = lax.broadcasted_iota(jnp.int32, (1, 128), 1)
    packed_src = jnp.zeros((1, 128), jnp.int32)
    for i in range(mine):
        packed_src = jnp.where(src_lane == i, cluster_src[0, i], packed_src)
    all_src[0] = packed_src
    each(grp_order, lambda i: src_copy(i).start())
    loads[4].wait()
    for i in range(mine):
        alive = (grp * mine + i) < cluster_count[0]
        keep = jnp.where(alive, 1.0, 0.0)
        send_blocks[i] = (own_blocks[i].astype(F32) * keep).astype(BF)
    each(grp_order, lambda i: block_copy(i).start())
    all_blocks[0] = send_blocks[:, pl.ds(pl.multiple_of(grp * rslice, rslice), rslice), :]
    acc[...] = jnp.zeros_like(acc)
    for l in range(leaves):
        down[l] = dot(base[l], trans[l]).astype(BF)

    def near(a):
        here = pl.multiple_of(a * width, width)
        inner = pl.multiple_of((a - 2) * width, width)
        square = dot(feat_t[pl.ds(inner, width), :], feat[:, pl.ds(here, 3 * width)])
        close = lax.rsqrt(square).astype(BF)
        acc[:, pl.ds(here, 3 * width)] += dot(sig[:, pl.ds(here, width)], close)
        acc[:, pl.ds(here, width)] += dot(
            sig[:, pl.ds(here + width, 2 * width)], close[:, width:], ((1,), (1,)))

    def slice_sum():
        wait_all(reduce_in, n_grp, reduce_recv)
        pair[0] = jnp.sum(reduce_in[...].astype(F32), axis=0).astype(BF)
        pair_copy().start()

    def plane_out():
        pair_copy().wait_recv()
        one, two = pair[0].astype(F32), pair[1].astype(F32)
        low = jnp.where(core == 0, one, two)
        high = jnp.where(core == 0, two, one)
        up[0] = jnp.concatenate([low, high], axis=1).astype(BF)
        each(plane_order, lambda i: plane_copy(i).start())

    def to_smem():
        return pltpu.make_async_copy(all_src, src_smem, smem_sem)

    def fetch_src():
        wait_all(all_src, n_grp, src_recv)
        to_smem().start()

    def couple():
        to_smem().wait()
        wait_all(all_blocks, n_grp, block_recv)
        wait_all(up, chips, plane_recv)
        tiles = []
        for i in range(n_grp):
            for j in range(mine):
                src = src_smem[i, 0, j]
                from_x = lax.rem(chip_x + n_x - src // (2 * n_y), n_x)
                from_y = lax.rem(chip_y + n_y - lax.rem(src // 2, n_y), n_y)
                tile = up[from_x * n_y + from_y]
                upper = lax.rem(src, 2) == 0
                tiles.append(jnp.where(upper, tile[:, :rows], tile[:, rows:]))
        stacked = jnp.concatenate(
            [all_blocks[i, j] for i in range(n_grp) for j in range(mine)], axis=0)
        field_in[0] = dot(jnp.concatenate(tiles, axis=0), stacked, ((0,), (0,))).astype(BF)
        each(grp_order, lambda i: field_copy(i).start())

    def halo_arrive():
        for i in range(4):
            halo_copy(i).wait_recv()
        feat[:, 0:edge] = features(pts_halo[0])[0]
        feat[:, edge + cols :] = features(pts_halo[1])[0]

        @pl.when(rank_id == 0)
        def _():
            sig[:, 0:edge] = jnp.zeros((rows, edge), BF)

        @pl.when(rank_id == total - 1)
        def _():
            sig[:, edge + cols :] = jnp.zeros((rows, edge), BF)

    def events(a):
        if a == 2:
            slice_sum()
        if a == 3:
            ring_pass(1, 0)
            plane_out()
            ring_pass(1, 1)
            fetch_src()
            for i in range(4):
                halo_copy(i).start()
        if a == 5:
            ring_pass(2, 0)
        if a == 6:
            ring_pass(2, 1)
        if a == 7:
            couple()
        if a == 8:
            ring_pass(3, 0)
            ring_pass(3, 1)

    def near_step(a, carry):
        @pl.when(a == leaves)
        def _():
            halo_arrive()

        near(a)
        for at in range(2, 9):
            @pl.when(a == at)
            def _():
                events(at)
        return carry

    lax.fori_loop(2, 2 + leaves, near_step, 0)
    square = dot(feat_t[0 : 2 * width, :], feat[:, 0:edge])
    close = lax.rsqrt(square).astype(BF)
    acc[:, edge : edge + width] += dot(sig[:, 0:edge], close[:width], ((1,), (1,)))
    acc[:, edge + width : edge + 2 * width] += dot(
        sig[:, width:edge], close[width:, width:], ((1,), (1,)))

    scale = 0.5 / math.sqrt(extent)
    wait_all(field_in, n_grp, field_recv)
    top = jnp.sum(field_in[...].astype(F32), axis=0).astype(BF)
    for l in range(leaves):
        cells = pl.ds(edge + l * width, width)
        acc[:, cells] = acc[:, cells] * scale + dot(top, down[l], ((1,), (1,)))

    loads[5].wait()
    loads[7].wait()
    loads[8].wait()
    ring_arrive(half - 1, 0)
    ring_arrive(half - 1, 1)
    for l in range(leaves):
        tiles = []
        for k in range(slots):
            src = leaf_src[l, k]
            tile = coefs[src // leaves, lax.rem(src, leaves)]
            tiles.append(jnp.where(k < leaf_count[l], tile, jnp.zeros_like(tile)))
        weights = blocks[l].reshape(slots * rank, rank)
        leaf_field = dot(jnp.concatenate(tiles, axis=1), weights).astype(BF)
        far_part = dot(leaf_field, base[l], ((1,), (1,)))
        near_part = acc[:, edge + l * width : edge + (l + 1) * width]
        out[:, l * width : (l + 1) * width] = (near_part + far_part).astype(BF)

    for i in range(4):
        halo_copy(i).wait_send()
    for step in range(half):
        for chunk in range(2):
            ring_sent(step, chunk)
    wait_all(all_blocks, n_grp, block_send)
    wait_all(all_src, n_grp, src_send)
    wait_all(reduce_in, n_grp, reduce_send)
    pair_copy().wait_send()
    wait_all(up, chips, plane_send)
    wait_all(field_in, n_grp, field_send)


def shards(n_leaf, n_grp, n_x, signal, points, basis, transfer, leaf_src, leaf_count,
           leaf_blocks, cluster_src, cluster_count, cluster_blocks):
    rows, cols = signal.shape
    leaves, width, rank = basis.shape
    mine = cluster_blocks.shape[1]
    slots = leaf_blocks.shape[1]
    rslice = rank // n_grp
    half = n_grp // 2
    ext = cols + 4 * width
    dma = pltpu.SemaphoreType.DMA
    hbm = pl.BlockSpec(memory_space=pltpu.HBM)
    operands = [pltpu.with_memory_space_constraint(v, pltpu.HBM) for v in (
        signal, points, basis, transfer, leaf_src, leaf_count, leaf_blocks,
        cluster_src, cluster_blocks[0])]
    operands.insert(8, cluster_count)
    smem = pl.BlockSpec(memory_space=pltpu.SMEM)
    vmem = pl.BlockSpec(memory_space=pltpu.VMEM)
    return pl.pallas_call(
        functools.partial(kernel, n_leaf, n_grp, n_x),
        out_shape=jax.ShapeDtypeStruct((rows, cols), BF),
        in_specs=[hbm] * 8 + [smem, hbm],
        out_specs=vmem,
        scratch_shapes=[
            pltpu.SMEM(leaf_src.shape, jnp.int32),
            pltpu.SMEM(leaf_count.shape, jnp.int32),
            pltpu.SMEM(cluster_src.shape, jnp.int32),
            pltpu.VMEM((rows, ext), BF),
            pltpu.VMEM(points.shape, BF),
            pltpu.VMEM((2, 3, 2 * width), BF),
            pltpu.VMEM((16, ext), BF),
            pltpu.VMEM((cols, 16), BF),
            pltpu.VMEM((leaves, width, rank), BF),
            pltpu.VMEM((leaves, rank, rank), BF),
            pltpu.VMEM((leaves, slots, rank, rank), BF),
            pltpu.VMEM((n_grp, leaves, rows, rank), BF),
            pltpu.VMEM((rows, ext), F32),
            pltpu.VMEM((rank, rows), BF),
            pltpu.VMEM((n_grp, rslice, rows), BF),
            pltpu.VMEM((2, rslice, rows), BF),
            pltpu.VMEM((n_leaf // 2, rslice, 2 * rows), BF),
            pltpu.VMEM((mine, rank, rank), BF),
            pltpu.VMEM((mine, rank, rank), BF),
            pltpu.VMEM((n_grp, mine, rslice, rank), BF),
            pltpu.VMEM((n_grp, 1, 128), jnp.int32),
            pltpu.SMEM((n_grp, 1, 128), jnp.int32),
            pltpu.VMEM((n_grp, rows, rank), BF),
            pltpu.VMEM((leaves, width, rank), BF),
            dma((10,)),
            dma((4,)), dma((4,)),
            dma((2, half, 2)), dma((2, half, 2)),
            dma, dma, dma, dma, dma, dma, dma, dma, dma, dma, dma, dma, dma,
        ],
        compiler_params=pltpu.CompilerParams(
            collective_id=0, has_side_effects=True, vmem_limit_bytes=VMEM_LIMIT),
        cost_estimate=pl.CostEstimate(
            flops=2 * rows * cols * 6 * width, bytes_accessed=6 * 1024 * 1024,
            transcendentals=3 * cols * width),
        name="h2_product",
    )(*operands)


def solution(mesh):
    both = ("leaf", "grp")
    placed = (
        P(None, both),
        P(None, both),
        P(both, None, None),
        P(both, None, None),
        P(both, None),
        P(both),
        P(both, None, None, None),
        P("leaf", "grp"),
        P("leaf"),
        P("leaf", "grp", None, None),
    )
    n_leaf, n_grp = mesh.shape["leaf"], mesh.shape["grp"]
    n_x = 4 if n_leaf == 64 else 2
    return jax.shard_map(
        functools.partial(shards, n_leaf, n_grp, n_x),
        mesh=mesh, in_specs=placed, out_specs=P(None, both), check_vma=False)
```

```python
import functools
import math

import jax
import jax.numpy as jnp
from jax import lax
from jax.experimental import pallas as pl
from jax.experimental.pallas import tpu as pltpu
from jax.sharding import PartitionSpec as P

BF = jnp.bfloat16
F32 = jnp.float32
MESH = pl.DeviceIdType.MESH
SOFTENING = 0.0025


def split3(value):
    first = value.astype(BF).astype(F32)
    rest = value - first
    second = rest.astype(BF).astype(F32)
    return first, second, rest - second


def dot(a, b, contract=((1,), (0,))):
    return lax.dot_general(a, b, (contract, ((), ())), preferred_element_type=F32)
VMEM_LIMIT = 48 * 1024 * 1024


def kernel(
    n_leaf, n_grp, n_x,
    signal, points, basis, transfer, leaf_src_in, leaf_count_in, leaf_blocks,
    cluster_src_in, cluster_count, cluster_blocks,
    out,
    leaf_src, leaf_count, cluster_src,
    sig, pts_in, pts_halo, feat, feat_t, base, trans, blocks, coefs, acc,
    part_t, reduce_in, pair, up, own_blocks, send_blocks, all_blocks,
    all_src, src_smem, field_in, down,
    load_sem, halo_send, halo_recv, ring_send, ring_recv,
    block_send, block_recv, src_send, src_recv, reduce_send, reduce_recv,
    pair_send, pair_recv, plane_send, plane_recv, field_send, field_recv, smem_sem,
):
    leaf = lax.axis_index("leaf")
    grp = lax.axis_index("grp")
    rows, cols = signal.shape
    leaves, width, rank = basis.shape
    slots = leaf_blocks.shape[1]
    mine = cluster_blocks.shape[0]
    rslice = rank // n_grp
    half = n_grp // 2
    n_y = n_leaf // (2 * n_x)
    chips = n_x * n_y
    edge = 2 * width
    extent = 5 * width
    core = lax.rem(leaf, 2)
    chip_y = lax.rem(leaf // 2, n_y)
    chip_x = leaf // (2 * n_y)
    rank_id = leaf * n_grp + grp
    total = n_leaf * n_grp
    right_id = lax.rem(rank_id + 1, total)
    left_id = lax.rem(rank_id + total - 1, total)
    right = (right_id // n_grp, lax.rem(right_id, n_grp))
    left = (left_id // n_grp, lax.rem(left_id, n_grp))
    other = (leaf + 1 - 2 * core, grp)

    def grp_peer(i):
        return (leaf, lax.rem(grp + i, n_grp))

    def plane_peer(i):
        to_x = lax.rem(chip_x + i // n_y, n_x)
        to_y = lax.rem(chip_y + lax.rem(i, n_y), n_y)
        return ((to_x * n_y + to_y) * 2 + core, grp)

    def ring_distance(i, n):
        return min(i % n, n - i % n)

    grp_order = sorted(range(1, n_grp), key=lambda i: -ring_distance(i, n_grp))
    plane_order = sorted(
        range(1, chips),
        key=lambda i: -ring_distance(i // n_y, n_x) - ring_distance(i % n_y, n_y))

    def each(order, fn):
        for i in order:
            fn(i)

    def remote(src, dst, send, recv, device):
        return pltpu.make_async_remote_copy(
            src, dst, send, recv, device_id=device, device_id_type=MESH)

    def wait_all(ref, n, sem):
        whole = ref.at[pl.ds(1, n - 1)]
        pltpu.make_async_copy(whole, whole, sem).wait()

    loads = [
        pltpu.make_async_copy(signal, sig.at[:, pl.ds(edge, cols)], load_sem.at[0]),
        pltpu.make_async_copy(basis, base, load_sem.at[1]),
        pltpu.make_async_copy(transfer, trans, load_sem.at[2]),
        pltpu.make_async_copy(points, pts_in, load_sem.at[3]),
        pltpu.make_async_copy(cluster_blocks, own_blocks, load_sem.at[4]),
        pltpu.make_async_copy(leaf_blocks, blocks, load_sem.at[5]),
        pltpu.make_async_copy(cluster_src_in, cluster_src, load_sem.at[6]),
        pltpu.make_async_copy(leaf_src_in, leaf_src, load_sem.at[8]),
        pltpu.make_async_copy(leaf_count_in, leaf_count, load_sem.at[9]),
    ]
    for load in loads[:5] + loads[6:]:
        load.start()

    barrier = pltpu.get_barrier_semaphore()

    def greet(device):
        pl.semaphore_signal(barrier, inc=1, device_id=device, device_id_type=MESH)

    each(plane_order, lambda i: greet(plane_peer(i)))
    each(grp_order, lambda i: greet(grp_peer(i)))
    greet(left)
    greet(right)
    greet(other)

    def halo_copy(i):
        return [
            lambda: remote(signal.at[:, pl.ds(cols - edge, edge)], sig.at[:, pl.ds(0, edge)],
                           halo_send.at[0], halo_recv.at[0], right),
            lambda: remote(signal.at[:, pl.ds(0, edge)], sig.at[:, pl.ds(edge + cols, edge)],
                           halo_send.at[1], halo_recv.at[1], left),
            lambda: remote(points.at[:, pl.ds(cols - edge, edge)], pts_halo.at[0],
                           halo_send.at[2], halo_recv.at[2], right),
            lambda: remote(points.at[:, pl.ds(0, edge)], pts_halo.at[1],
                           halo_send.at[3], halo_recv.at[3], left),
        ][i]()

    def block_copy(i):
        target = grp_peer(i)
        return remote(
            send_blocks.at[:, pl.ds(pl.multiple_of(target[1] * rslice, rslice), rslice), :],
            all_blocks.at[i], block_send, block_recv, target)

    def src_copy(i):
        return remote(all_src.at[0], all_src.at[i], src_send, src_recv, grp_peer(i))

    def reduce_copy(i):
        target = grp_peer(i)
        return remote(
            part_t.at[pl.ds(pl.multiple_of(target[1] * rslice, rslice), rslice), :],
            reduce_in.at[i], reduce_send, reduce_recv, target)

    def pair_copy():
        return remote(pair.at[0], pair.at[1], pair_send, pair_recv, other)

    def plane_copy(i):
        return remote(up.at[0], up.at[i], plane_send, plane_recv, plane_peer(i))

    def field_copy(i):
        return remote(field_in.at[0], field_in.at[i], field_send, field_recv, grp_peer(i))

    def ring_copy(side, step, chunk, slot):
        target = grp_peer(1) if side == 0 else grp_peer(n_grp - 1)
        ref = coefs.at[slot, pl.ds(chunk * (leaves // 2), leaves // 2)]
        return remote(ref, ref, ring_send.at[side, step, chunk],
                      ring_recv.at[side, step, chunk], target)

    def ring_sides(step, chunk):
        return (0, 1) if step < half - 1 else (chunk,)

    def ring_start(step, chunk):
        for side in ring_sides(step, chunk):
            away = n_grp - step if side == 0 else step
            ring_copy(side, step, chunk, lax.rem(grp + away, n_grp)).start()

    def ring_arrive(step, chunk):
        for side in ring_sides(step, chunk):
            away = n_grp - step - 1 if side == 0 else step + 1
            ring_copy(side, step, chunk, lax.rem(grp + away, n_grp)).wait_recv()

    def ring_sent(step, chunk):
        for side in ring_sides(step, chunk):
            away = n_grp - step if side == 0 else step
            ring_copy(side, step, chunk, lax.rem(grp + away, n_grp)).wait_send()

    def ring_pass(step, chunk):
        if step < half:
            ring_arrive(step - 1, chunk)
            ring_start(step, chunk)

    loads[0].wait()
    loads[1].wait()
    loads[5].start()
    for l in range(leaves):
        first = edge + l * width
        coefs[grp, l] = dot(sig[:, first : first + width], base[l]).astype(BF)
    loads[2].wait()
    upward = jnp.zeros((rows, rank), F32)
    for l in range(leaves):
        upward = upward + dot(coefs[grp, l], trans[l])
    part_t[...] = upward.T.astype(BF)
    pl.semaphore_wait(barrier, n_grp - 1 + chips - 1 + 3)
    each(grp_order, lambda i: reduce_copy(i).start())
    ring_start(0, 0)
    ring_start(0, 1)
    reduce_in[0] = part_t[pl.ds(pl.multiple_of(grp * rslice, rslice), rslice), :]

    def features(cells):
        pts = cells.astype(F32)
        n = pts.shape[1]
        norm = pts[0:1] * pts[0:1] + pts[1:2] * pts[1:2] + pts[2:3] * pts[2:3]
        pieces = jnp.concatenate(split3(norm), axis=0)
        ones = jnp.ones((3, n), F32)
        soft = jnp.concatenate(split3(jnp.full((1, n), SOFTENING, F32)), axis=0)
        fill = jnp.zeros((4, n), F32)
        one = jnp.concatenate([-2.0 * pts, ones, pieces, ones, fill], axis=0).astype(BF)
        return one, jnp.concatenate([pts, pieces, ones, soft, fill], axis=0)

    loads[3].wait()
    here_feat, here_other = features(pts_in[...])
    feat[:, edge : edge + cols] = here_feat
    feat_t[...] = here_other.T.astype(BF)

    loads[6].wait()
    src_lane = lax.broadcasted_iota(jnp.int32, (1, 128), 1)
    packed_src = jnp.zeros((1, 128), jnp.int32)
    for i in range(mine):
        packed_src = jnp.where(src_lane == i, cluster_src[0, i], packed_src)
    all_src[0] = packed_src
    each(grp_order, lambda i: src_copy(i).start())
    loads[4].wait()
    for i in range(mine):
        alive = (grp * mine + i) < cluster_count[0]
        keep = jnp.where(alive, 1.0, 0.0)
        send_blocks[i] = (own_blocks[i].astype(F32) * keep).astype(BF)
    each(grp_order, lambda i: block_copy(i).start())
    all_blocks[0] = send_blocks[:, pl.ds(pl.multiple_of(grp * rslice, rslice), rslice), :]
    acc[...] = jnp.zeros_like(acc)
    for l in range(leaves):
        down[l] = dot(base[l], trans[l]).astype(BF)

    def near(a):
        here = pl.multiple_of(a * width, width)
        inner = pl.multiple_of((a - 2) * width, width)
        square = dot(feat_t[pl.ds(inner, width), :], feat[:, pl.ds(here, 3 * width)])
        close = lax.rsqrt(square).astype(BF)
        acc[:, pl.ds(here, 3 * width)] += dot(sig[:, pl.ds(here, width)], close)
        acc[:, pl.ds(here, width)] += dot(
            sig[:, pl.ds(here + width, 2 * width)], close[:, width:], ((1,), (1,)))

    def slice_sum():
        wait_all(reduce_in, n_grp, reduce_recv)
        pair[0] = jnp.sum(reduce_in[...].astype(F32), axis=0).astype(BF)
        pair_copy().start()

    def plane_out():
        pair_copy().wait_recv()
        one, two = pair[0].astype(F32), pair[1].astype(F32)
        low = jnp.where(core == 0, one, two)
        high = jnp.where(core == 0, two, one)
        up[0] = jnp.concatenate([low, high], axis=1).astype(BF)
        each(plane_order, lambda i: plane_copy(i).start())

    def to_smem():
        return pltpu.make_async_copy(all_src, src_smem, smem_sem)

    def fetch_src():
        wait_all(all_src, n_grp, src_recv)
        to_smem().start()

    def couple():
        to_smem().wait()
        wait_all(all_blocks, n_grp, block_recv)
        wait_all(up, chips, plane_recv)
        tiles = []
        for i in range(n_grp):
            for j in range(mine):
                src = src_smem[i, 0, j]
                from_x = lax.rem(chip_x + n_x - src // (2 * n_y), n_x)
                from_y = lax.rem(chip_y + n_y - lax.rem(src // 2, n_y), n_y)
                tile = up[from_x * n_y + from_y]
                upper = lax.rem(src, 2) == 0
                tiles.append(jnp.where(upper, tile[:, :rows], tile[:, rows:]))
        stacked = jnp.concatenate(
            [all_blocks[i, j] for i in range(n_grp) for j in range(mine)], axis=0)
        field_in[0] = dot(jnp.concatenate(tiles, axis=0), stacked, ((0,), (0,))).astype(BF)
        each(grp_order, lambda i: field_copy(i).start())

    def halo_arrive():
        for i in range(4):
            halo_copy(i).wait_recv()
        feat[:, 0:edge] = features(pts_halo[0])[0]
        feat[:, edge + cols :] = features(pts_halo[1])[0]

        @pl.when(rank_id == 0)
        def _():
            sig[:, 0:edge] = jnp.zeros((rows, edge), BF)

        @pl.when(rank_id == total - 1)
        def _():
            sig[:, edge + cols :] = jnp.zeros((rows, edge), BF)

    def events(a):
        if a == 2:
            slice_sum()
        if a == 3:
            ring_pass(1, 0)
            plane_out()
            ring_pass(1, 1)
            fetch_src()
            for i in range(4):
                halo_copy(i).start()
        if a == 5:
            ring_pass(2, 0)
        if a == 6:
            ring_pass(2, 1)
        if a == 7:
            couple()
            ring_pass(3, 0)
            ring_pass(3, 1)

    def near_step(a, carry):
        @pl.when(a == leaves)
        def _():
            halo_arrive()

        near(a)
        for at in range(2, 8):
            @pl.when(a == at)
            def _():
                events(at)
        return carry

    lax.fori_loop(2, 2 + leaves, near_step, 0)
    square = dot(feat_t[0 : 2 * width, :], feat[:, 0:edge])
    close = lax.rsqrt(square).astype(BF)
    acc[:, edge : edge + width] += dot(sig[:, 0:edge], close[:width], ((1,), (1,)))
    acc[:, edge + width : edge + 2 * width] += dot(
        sig[:, width:edge], close[width:, width:], ((1,), (1,)))

    scale = 0.5 / math.sqrt(extent)
    wait_all(field_in, n_grp, field_recv)
    top = jnp.sum(field_in[...].astype(F32), axis=0).astype(BF)
    for l in range(leaves):
        cells = pl.ds(edge + l * width, width)
        acc[:, cells] = acc[:, cells] * scale + dot(top, down[l], ((1,), (1,)))

    loads[5].wait()
    loads[7].wait()
    loads[8].wait()
    ring_arrive(half - 1, 0)
    ring_arrive(half - 1, 1)
    for l in range(leaves):
        tiles = []
        for k in range(slots):
            src = leaf_src[l, k]
            tile = coefs[src // leaves, lax.rem(src, leaves)]
            tiles.append(jnp.where(k < leaf_count[l], tile, jnp.zeros_like(tile)))
        weights = blocks[l].reshape(slots * rank, rank)
        leaf_field = dot(jnp.concatenate(tiles, axis=1), weights).astype(BF)
        far_part = dot(leaf_field, base[l], ((1,), (1,)))
        near_part = acc[:, edge + l * width : edge + (l + 1) * width]
        out[:, l * width : (l + 1) * width] = (near_part + far_part).astype(BF)

    for i in range(4):
        halo_copy(i).wait_send()
    for step in range(half):
        for chunk in range(2):
            ring_sent(step, chunk)
    wait_all(all_blocks, n_grp, block_send)
    wait_all(all_src, n_grp, src_send)
    wait_all(reduce_in, n_grp, reduce_send)
    pair_copy().wait_send()
    wait_all(up, chips, plane_send)
    wait_all(field_in, n_grp, field_send)


def shards(n_leaf, n_grp, n_x, signal, points, basis, transfer, leaf_src, leaf_count,
           leaf_blocks, cluster_src, cluster_count, cluster_blocks):
    rows, cols = signal.shape
    leaves, width, rank = basis.shape
    mine = cluster_blocks.shape[1]
    slots = leaf_blocks.shape[1]
    rslice = rank // n_grp
    half = n_grp // 2
    ext = cols + 4 * width
    dma = pltpu.SemaphoreType.DMA
    hbm = pl.BlockSpec(memory_space=pltpu.HBM)
    operands = [pltpu.with_memory_space_constraint(v, pltpu.HBM) for v in (
        signal, points, basis, transfer, leaf_src, leaf_count, leaf_blocks,
        cluster_src, cluster_blocks[0])]
    operands.insert(8, cluster_count)
    smem = pl.BlockSpec(memory_space=pltpu.SMEM)
    vmem = pl.BlockSpec(memory_space=pltpu.VMEM)
    return pl.pallas_call(
        functools.partial(kernel, n_leaf, n_grp, n_x),
        out_shape=jax.ShapeDtypeStruct((rows, cols), BF),
        in_specs=[hbm] * 8 + [smem, hbm],
        out_specs=vmem,
        scratch_shapes=[
            pltpu.SMEM(leaf_src.shape, jnp.int32),
            pltpu.SMEM(leaf_count.shape, jnp.int32),
            pltpu.SMEM(cluster_src.shape, jnp.int32),
            pltpu.VMEM((rows, ext), BF),
            pltpu.VMEM(points.shape, BF),
            pltpu.VMEM((2, 3, 2 * width), BF),
            pltpu.VMEM((16, ext), BF),
            pltpu.VMEM((cols, 16), BF),
            pltpu.VMEM((leaves, width, rank), BF),
            pltpu.VMEM((leaves, rank, rank), BF),
            pltpu.VMEM((leaves, slots, rank, rank), BF),
            pltpu.VMEM((n_grp, leaves, rows, rank), BF),
            pltpu.VMEM((rows, ext), F32),
            pltpu.VMEM((rank, rows), BF),
            pltpu.VMEM((n_grp, rslice, rows), BF),
            pltpu.VMEM((2, rslice, rows), BF),
            pltpu.VMEM((n_leaf // 2, rslice, 2 * rows), BF),
            pltpu.VMEM((mine, rank, rank), BF),
            pltpu.VMEM((mine, rank, rank), BF),
            pltpu.VMEM((n_grp, mine, rslice, rank), BF),
            pltpu.VMEM((n_grp, 1, 128), jnp.int32),
            pltpu.SMEM((n_grp, 1, 128), jnp.int32),
            pltpu.VMEM((n_grp, rows, rank), BF),
            pltpu.VMEM((leaves, width, rank), BF),
            dma((10,)),
            dma((4,)), dma((4,)),
            dma((2, half, 2)), dma((2, half, 2)),
            dma, dma, dma, dma, dma, dma, dma, dma, dma, dma, dma, dma, dma,
        ],
        compiler_params=pltpu.CompilerParams(
            collective_id=0, has_side_effects=True, vmem_limit_bytes=VMEM_LIMIT),
        cost_estimate=pl.CostEstimate(
            flops=2 * rows * cols * 6 * width, bytes_accessed=6 * 1024 * 1024,
            transcendentals=3 * cols * width),
        name="h2_product",
    )(*operands)


def solution(mesh):
    both = ("leaf", "grp")
    placed = (
        P(None, both),
        P(None, both),
        P(both, None, None),
        P(both, None, None),
        P(both, None),
        P(both),
        P(both, None, None, None),
        P("leaf", "grp"),
        P("leaf"),
        P("leaf", "grp", None, None),
    )
    n_leaf, n_grp = mesh.shape["leaf"], mesh.shape["grp"]
    n_x = 4 if n_leaf == 64 else 2
    return jax.shard_map(
        functools.partial(shards, n_leaf, n_grp, n_x),
        mesh=mesh, in_specs=placed, out_specs=P(None, both), check_vma=False)
```
